128 devices in a mesh: row: 8 (over z, x_lo), col: 16 (over x_hi, y, core).
Axes of the slice: x: 4 (x_hi: 2, x_lo: 2; x = x_hi * 2 + x_lo), y: 4, z: 4, core: 2. Of those that a mesh axis runs over, the one named last changes fastest.
Arguments:
- eigen_basis_rows: float32 [16384, 8192], P('row', 'col'), may hold values from -6 to 6
- mirror_entries: float32 [6, 8, 128, 2176], P(None, 'row', 'col'), may hold values from -0.125 to 0.125
- tau_coefficients: float32 [6, 8, 128], P(None, 'row', 'col'), may hold values from 0.5 to 2
- mirror_tallies: int32 [6, 8], P(None, 'row'), may hold values from 32 to 128
Outputs:
- transformed: float32 [16384, 8192], P('row', 'col')
The draws below stay inside these ranges and needn't reach their ends.
All inputs are finite; a program needn't handle non-finite values.
Results may differ from the reference program's by a relative error of at most 0.00017.
Values sent between devices are 32-bit elements; how exact they have to be, the bound alone decides.
A program may use at most 64 MiB of HBM per device.

```python
import math
import jax
import jax.numpy as jnp
from jax import lax

PANEL_EXTENT = 128
R_DEV = 2048
MIRROR_BATCHES = 6
WIN = 2176
ROWS = 16384
COLS = 8192
N_ROW = 8


def set_ends(array, key, smallest, high):
    extent = array.shape
    index_at = [jax.random.randint(jax.random.fold_in(key, axis), (), 0, extent[axis]) for axis in range(len(extent))]
    array = array.at[tuple(index_at)].set(smallest)
    longest = extent.index(max(extent))
    index_at[longest] = (index_at[longest] + 1) % extent[longest]
    return array.at[tuple(index_at)].set(high)


def levels(own_key, extent, pieces, low, top_value):
    def one(position, blocks):
        heights = jax.random.uniform(jax.random.fold_in(jax.random.fold_in(own_key, 6), position), (blocks,), jnp.float32, low / len(pieces), top_value / len(pieces))
        return jnp.repeat(jnp.exp(heights), extent[position] // blocks).reshape((-1,) + (1,) * (len(extent) - position - 1))

    factor_of = one(*pieces[0])
    for cut in pieces[1:]:
        factor_of = factor_of * one(*cut)
    return factor_of


def centred(own_key, shape, width, reach, split=(), kind=jnp.bfloat16):
    drawn = width * jax.random.normal(own_key, shape, jnp.float32)
    if split:
        drawn = drawn * levels(own_key, shape, split, -0.22, 0.18)
    return jnp.clip(drawn, -reach, reach).astype(kind)


def setup_inputs(seed: int = 0) -> dict:
    seeds = jax.random.split(jax.random.key(seed), 5)
    return {
        "eigen_basis_rows": centred(seeds[0], (ROWS, COLS), 1.0, 6.0, ((0, 8), (1, 16)), jnp.float32),
        "mirror_entries": centred(seeds[1], (MIRROR_BATCHES, N_ROW, PANEL_EXTENT, WIN), WIN ** -0.5, 0.125, ((1, 8), (2, 16)), jnp.float32),
        "tau_coefficients": jnp.clip(jnp.exp(math.log(2.0) - 1.3862944 * jax.random.uniform(seeds[2], (MIRROR_BATCHES, N_ROW, PANEL_EXTENT), jnp.float32) ** levels(seeds[2], (MIRROR_BATCHES, N_ROW, PANEL_EXTENT), ((1, 8), (2, 16)), -0.2, 0.2)), 0.5, 2.0),
        "mirror_tallies": set_ends(jax.random.randint(seeds[3], (MIRROR_BATCHES, N_ROW), PANEL_EXTENT // 4, PANEL_EXTENT + 1), jax.random.fold_in(seeds[3], 1), PANEL_EXTENT // 4, PANEL_EXTENT).astype(jnp.int32),
    }


PRECISE = lax.Precision.HIGHEST


def storage_triangle(mirror_directions, scaling, retention_flags):
    gram_matrix = lax.dot_general(mirror_directions, mirror_directions, (((1,), (1,)), ((), ())), precision=PRECISE, preferred_element_type=jnp.float32)
    diag_inverse = jnp.where(retention_flags, scaling, jnp.ones_like(scaling))
    nilpotent = diag_inverse[:, None] * jnp.triu(gram_matrix, 1)
    order_count = mirror_directions.shape[0]
    identity = jnp.eye(order_count, dtype=jnp.float32)
    power_term = -nilpotent
    inverse_part = identity + power_term
    reached = 1
    while 2 * reached < order_count:
        power_term = jnp.dot(power_term, power_term, precision=PRECISE, preferred_element_type=jnp.float32)
        inverse_part = inverse_part + jnp.dot(inverse_part, power_term, precision=PRECISE, preferred_element_type=jnp.float32)
        reached = reached * 2
    return inverse_part * diag_inverse[None, :]


def apply_block(window, mirror_directions, triangle_operator):
    coeffs = jnp.dot(mirror_directions, window, precision=PRECISE, preferred_element_type=jnp.float32)
    mixed_terms = jnp.dot(triangle_operator, coeffs, precision=PRECISE, preferred_element_type=jnp.float32)
    return window - lax.dot_general(mirror_directions, mixed_terms, (((0,), (0,)), ((), ())), precision=PRECISE, preferred_element_type=jnp.float32)


def reference(eigen_basis_rows, mirror_entries, tau_coefficients, mirror_tallies):
    column_count = eigen_basis_rows.shape[1]
    padded = jnp.concatenate([eigen_basis_rows, jnp.zeros((PANEL_EXTENT, column_count), jnp.float32)], axis=0)
    slot_index = jnp.arange(PANEL_EXTENT, dtype=jnp.int32)
    cell_index = jnp.arange(WIN, dtype=jnp.int32)
    for batch_ordinal in range(MIRROR_BATCHES):
        for panel_ordinal in range(N_ROW):
            retention_flags = slot_index < mirror_tallies[batch_ordinal, panel_ordinal]
            if panel_ordinal == N_ROW - 1:
                row_keep = cell_index < R_DEV
            else:
                row_keep = cell_index >= 0
            mirror_directions = mirror_entries[batch_ordinal, panel_ordinal] * retention_flags[:, None].astype(jnp.float32) * row_keep[None, :].astype(jnp.float32)
            triangle_operator = storage_triangle(mirror_directions, tau_coefficients[batch_ordinal, panel_ordinal], retention_flags)
            first_row = panel_ordinal * R_DEV
            window = apply_block(padded[first_row:first_row + WIN], mirror_directions, triangle_operator)
            padded = padded.at[first_row:first_row + WIN].set(window)
    return padded[:N_ROW * R_DEV]
```

```python
import jax
import jax.numpy as jnp
from jax import lax
from jax.experimental import pallas as pl
from jax.experimental.pallas import tpu as pltpu
from jax.sharding import PartitionSpec as P

EXACT = lax.Precision.HIGHEST
THREE = lax.Precision.HIGH
MESH = pl.DeviceIdType.MESH
B = 128
NC = 4


def mm(a, b, precision, ca=1, cb=0):
    return lax.dot_general(
        a, b, (((ca,), (cb,)), ((), ())), precision=precision, preferred_element_type=jnp.float32
    )


def bmm(a, b, ca=2, cb=1):
    return lax.dot_general(
        a, b, (((ca,), (cb,)), ((0,), (0,))), precision=EXACT, preferred_element_type=jnp.float32
    )


def factors_of(gram, scale, live):
    diag = jnp.where(live, scale, jnp.ones_like(scale))
    power = -(diag[:, :, None] * jnp.triu(gram, 1))
    order = gram.shape[1]
    inverse = jnp.eye(order, dtype=jnp.float32)[None] + power
    reached = 1
    while 2 * reached < order:
        power = bmm(power, power)
        inverse = inverse + bmm(inverse, power)
        reached = reached * 2
    return inverse * diag[:, None, :]


def chain_kernel(
    xh, pm, gc, tb, e, f, c_out, head_out, y, ty, hin, hout, xs, own, s_up0, s_up, s_dn, r_h, r_t
):
    groups = pm.shape[0]
    width = hin.shape[-1]
    chunks = hin.shape[1]
    row = lax.axis_index("row")
    rows = lax.axis_size("row")
    first = row == 0
    last = row == rows - 1

    bar = pltpu.get_barrier_semaphore()

    @pl.when(jnp.logical_not(first))
    def _():
        pl.semaphore_signal(bar, inc=1, device_id={"row": row - 1}, device_id_type=MESH)

    @pl.when(jnp.logical_not(last))
    def _():
        pl.semaphore_signal(bar, inc=1, device_id={"row": row + 1}, device_id_type=MESH)

    @pl.when(first | last)
    def _():
        pl.semaphore_wait(bar, 1)

    @pl.when(jnp.logical_not(first | last))
    def _():
        pl.semaphore_wait(bar, 2)

    def up0(k):
        return pltpu.make_async_remote_copy(
            src_ref=xs.at[k],
            dst_ref=hin.at[0, k, pl.ds(B, B)],
            send_sem=s_up0.at[k],
            recv_sem=r_t.at[0, k],
            device_id={"row": row - 1},
            device_id_type=MESH,
        )

    def up(g, k):
        return pltpu.make_async_remote_copy(
            src_ref=hout.at[g, k, pl.ds(0, B)],
            dst_ref=hin.at[g + 1, k, pl.ds(B, B)],
            send_sem=s_up.at[g, k],
            recv_sem=r_t.at[g + 1, k],
            device_id={"row": row - 1},
            device_id_type=MESH,
        )

    def down(g, k):
        return pltpu.make_async_remote_copy(
            src_ref=hout.at[g, k, pl.ds(B, B)],
            dst_ref=hin.at[g, k, pl.ds(0, B)],
            send_sem=s_dn.at[g, k],
            recv_sem=r_h.at[g, k],
            device_id={"row": row + 1},
            device_id_type=MESH,
        )

    def recv_h(g, k):
        return pltpu.make_async_remote_copy(
            src_ref=hout.at[g, k, pl.ds(B, B)],
            dst_ref=hin.at[g, k, pl.ds(0, B)],
            send_sem=s_dn.at[g, k],
            recv_sem=r_h.at[g, k],
            device_id={"row": row - 1},
            device_id_type=MESH,
        )

    def recv_t(g, k):
        return pltpu.make_async_remote_copy(
            src_ref=xs.at[k],
            dst_ref=hin.at[g, k, pl.ds(B, B)],
            send_sem=s_up0.at[k],
            recv_sem=r_t.at[g, k],
            device_id={"row": row + 1},
            device_id_type=MESH,
        )

    for k in range(chunks):
        xs[k] = xh[:, k * width : (k + 1) * width]
        own[k] = xs[k]

    @pl.when(jnp.logical_not(first))
    def _():
        for k in range(chunks):
            up0(k).start()

    @pl.when(last)
    def _():
        for g in range(groups):
            for k in range(chunks):
                hin[g, k, B:] = jnp.zeros((B, width), jnp.float32)

    y[...] = pm[...]
    ty[...] = mm(tb[0], pm[0], THREE)

    def step(g, carry):
        for k in range(chunks):
            cols = slice(k * width, (k + 1) * width)

            @pl.when(jnp.logical_not(first))
            def _():
                recv_h(g, k).wait_recv()

            @pl.when(jnp.logical_not(last))
            def _():
                recv_t(g, k).wait_recv()

            top = jnp.where(first, own[k], hin[g, k, :B])
            h = jnp.concatenate([top, hin[g, k, B:]], axis=0)
            hn = (h - ty[B:, cols]) - mm(f[g], h, THREE)
            hout[g, k] = hn

            @pl.when(jnp.logical_not(last))
            def _():
                down(g, k).start()

            @pl.when(jnp.logical_not(first) & (g < groups - 1))
            def _():
                up(g, k).start()

            own[k] = hn[:B]
            c_out[g, :, cols] = ty[:B, cols] + mm(e[g], h, THREE)

        @pl.when(g < groups - 1)
        def _():
            change = mm(gc[g], c_out[g], THREE)
            y[...] = y[...] - change.reshape(y.shape)
            ty[...] = mm(tb[g + 1], y[g + 1], THREE)

        return carry

    lax.fori_loop(0, groups, step, 0)
    for k in range(chunks):
        head_out[:, k * width : (k + 1) * width] = hout[groups - 1, k, :B]

    @pl.when(jnp.logical_not(first))
    def _():
        for k in range(chunks):
            up0(k).wait_send()

        def drain(g, carry):
            for k in range(chunks):
                up(g, k).wait_send()
            return carry

        lax.fori_loop(0, groups - 1, drain, 0)

    @pl.when(jnp.logical_not(last))
    def _():
        def drain(g, carry):
            for k in range(chunks):
                down(g, k).wait_send()
            return carry

        lax.fori_loop(0, groups, drain, 0)


def chain(xh, pm, gc, tb, e, f):
    groups, _, columns = pm.shape
    width = columns // NC
    vm = pl.BlockSpec(memory_space=pltpu.VMEM)
    f32 = jnp.float32
    return pl.pallas_call(
        chain_kernel,
        out_shape=(
            jax.ShapeDtypeStruct((groups, B, columns), f32),
            jax.ShapeDtypeStruct((B, columns), f32),
        ),
        in_specs=[vm] * 6,
        out_specs=(vm, vm),
        scratch_shapes=[
            pltpu.VMEM((groups, B, columns), f32),
            pltpu.VMEM((3 * B, columns), f32),
            pltpu.VMEM((groups, NC, 2 * B, width), f32),
            pltpu.VMEM((groups, NC, 2 * B, width), f32),
            pltpu.VMEM((NC, B, width), f32),
            pltpu.VMEM((NC, B, width), f32),
            pltpu.SemaphoreType.DMA((NC,)),
            pltpu.SemaphoreType.DMA((groups, NC)),
            pltpu.SemaphoreType.DMA((groups, NC)),
            pltpu.SemaphoreType.DMA((groups, NC)),
            pltpu.SemaphoreType.DMA((groups, NC)),
        ],
        compiler_params=pltpu.CompilerParams(
            collective_id=0, has_side_effects=True, vmem_limit_bytes=40 << 20
        ),
        name="chain",
    )(xh, pm, gc, tb, e, f)


def per_device(x, mirror_entries, tau, tallies):
    v = lax.all_gather(mirror_entries, "col", axis=2, tiled=True)[:, 0]
    scale = lax.all_gather(tau, "col", axis=2, tiled=True)[:, 0]
    counts = tallies[:, 0]
    row_count, columns = x.shape
    groups, width, window = v.shape
    position = lax.axis_index("row")
    sections = lax.axis_size("row")
    live = lax.iota(jnp.int32, width)[None, :] < counts[:, None]
    keep = (lax.iota(jnp.int32, window) < row_count) | (position != sections - 1)
    v = v * live[:, :, None].astype(jnp.float32) * keep[None, None, :].astype(jnp.float32)
    w = jnp.concatenate([v[:, :, :B], v[:, :, row_count:]], axis=2)
    mid = v.reshape(groups * width, window)[:, B:row_count]
    xm = x[B:]
    pm = mm(mid, xm, THREE).reshape(groups, width, columns)
    gm = mm(mid, mid, THREE, 1, 1).reshape(groups, width, groups, width)
    gd = jnp.stack([gm[g, :, g] for g in range(groups)]) + bmm(w, w, 2, 2)
    tf = factors_of(gd, scale, live)
    e = bmm(tf, w)
    b = bmm(w, tf, 1, 1)
    f = bmm(b, w)
    tb = jnp.concatenate([tf, b], axis=1)
    below = jnp.arange(groups)[:, None] > jnp.arange(groups)[None, :]
    gc = jnp.where(below[:, None, :, None], gm, 0.0).transpose(2, 0, 1, 3)
    gc = gc.reshape(groups, groups * width, width)
    c, head = chain(x[:B], pm, gc, tb, e, f)
    out_mid = xm - mm(mid, c.reshape(groups * width, columns), THREE, 0, 0)
    return jnp.concatenate([head, out_mid], axis=0)


def solution(mesh):
    in_specs = (P("row", "col"), P(None, "row", "col", None), P(None, "row", "col"), P(None, "row"))
    return jax.shard_map(
        per_device, mesh=mesh, in_specs=in_specs, out_specs=P("row", "col"), check_vma=False
    )
```

```python
import jax
import jax.numpy as jnp
from jax import lax
from jax.experimental import pallas as pl
from jax.experimental.pallas import tpu as pltpu
from jax.sharding import PartitionSpec as P

EXACT = lax.Precision.HIGHEST
THREE = lax.Precision.HIGH
MESH = pl.DeviceIdType.MESH
B = 128
NC = 4


def mm(a, b, precision, ca=1, cb=0):
    return lax.dot_general(
        a, b, (((ca,), (cb,)), ((), ())), precision=precision, preferred_element_type=jnp.float32
    )


def mdot(a, b, ca=1, cb=0):
    return lax.dot_general(a, b, (((ca,), (cb,)), ((), ())), preferred_element_type=jnp.float32)


def split(value):
    high = value.astype(jnp.bfloat16)
    return high, (value - high.astype(jnp.float32)).astype(jnp.bfloat16)


def prep_kernel(
    vin, live, x, vout, pm, gc, tb, e, f, vbuf, vh, vl, wbuf, gdbuf, xh, xl, s_sem, r_sem, o_sem
):
    groups, width, lanes = vbuf.shape
    window = lanes - B
    row_count = x.shape[0]
    half = lanes // 2
    row, col = lax.axis_index("row"), lax.axis_index("col")
    keep = (row != lax.axis_size("row") - 1).astype(jnp.float32)
    side, y, core = col // 8, (col % 8) // 2, col % 2

    def shard(side_, y_):
        return side_ * 8 + (y_ % 4) * 2 + core

    other = 1 - side
    to_up = shard(side, y + 1)
    to_down = shard(side, y + 3)
    to_x = shard(other, y)
    to_sib = col + 1 - 2 * core

    bar = pltpu.get_barrier_semaphore()
    for target in (to_up, to_down, to_x, to_sib):
        pl.semaphore_signal(bar, inc=1, device_id={"col": target}, device_id_type=MESH)

    def rows_of(owner):
        return pl.ds(pl.multiple_of(owner * 8, 8), 8)

    for g in range(groups):
        vbuf[g, rows_of(col), :] = vin[g]

    def copy(g, kind, owner, target, part=None):
        span = pl.ds(0, lanes) if part is None else pl.ds(part * half, half)
        place = vbuf.at[g, rows_of(owner), span]
        return pltpu.make_async_remote_copy(
            src_ref=place,
            dst_ref=place,
            send_sem=s_sem.at[g, kind],
            recv_sem=r_sem.at[g, kind],
            device_id={"col": target},
            device_id_type=MESH,
        )

    def sent(g, kind):
        owner, target, part = (
            (col, to_up, None),
            (col, to_down, None),
            (col, to_x, None),
            (shard(side, y + 3), to_up, 0),
            (shard(side, y + 1), to_down, 1),
            (shard(other, y), to_up, None),
            (shard(other, y), to_down, None),
            (shard(other, y + 3), to_up, 0),
            (shard(other, y + 1), to_down, 1),
        )[kind]
        return copy(g, kind, owner, target, part)

    def got(g, kind):
        owner, part = (
            (shard(side, y + 3), None),
            (shard(side, y + 1), None),
            (shard(other, y), None),
            (shard(side, y + 2), 0),
            (shard(side, y + 2), 1),
            (shard(other, y + 3), None),
            (shard(other, y + 1), None),
            (shard(other, y + 2), 0),
            (shard(other, y + 2), 1),
        )[kind]
        return copy(g, kind, owner, to_up, part)

    def relay(g, mine, step):
        owner = shard(side if mine else other, y + step)
        return copy(g, (9 if mine else 13) + step, owner, to_sib)

    def relayed(g, mine, step):
        owner = shard(side if mine else other, y + step) + 1 - 2 * core
        return copy(g, (9 if mine else 13) + step, owner, to_sib)

    def c0(g):
        for kind in (0, 1, 2):
            sent(g, kind).start()
        relay(g, True, 0).start()

    def c1(g):
        got(g, 0).wait_recv()
        sent(g, 3).start()
        relay(g, True, 3).start()
        got(g, 1).wait_recv()
        sent(g, 4).start()
        relay(g, True, 1).start()
        got(g, 2).wait_recv()
        sent(g, 5).start()
        sent(g, 6).start()
        relay(g, False, 0).start()

    def c2(g):
        got(g, 5).wait_recv()
        sent(g, 7).start()
        relay(g, False, 3).start()
        got(g, 6).wait_recv()
        sent(g, 8).start()
        relay(g, False, 1).start()
        got(g, 3).wait_recv()
        got(g, 4).wait_recv()
        relay(g, True, 2).start()

    def c3(g):
        got(g, 7).wait_recv()
        got(g, 8).wait_recv()
        relay(g, False, 2).start()

    def c4(g):
        for mine in (True, False):
            for step in range(4):
                relayed(g, mine, step).wait_recv()
        pltpu.make_async_copy(vbuf.at[g], vout.at[g], o_sem.at[g]).start()

    def products(g):
        alive = live[:, g : g + 1]
        mid = vbuf[g, :, B:row_count] * alive
        high, low = split(mid)
        at = slice(g * width, (g + 1) * width)
        vh[at] = high
        vl[at] = low
        wbuf[g, :, :B] = vbuf[g, :, :B] * alive
        wbuf[g, :, B:] = vbuf[g, :, row_count:window] * (alive * keep)
        high, low = vh[at], vl[at]
        pm[g] = mdot(high, xh[...]) + mdot(low, xh[...]) + mdot(high, xl[...])
        upto = slice(0, (g + 1) * width)
        gram = (
            mdot(high, vh[upto], 1, 1) + mdot(low, vh[upto], 1, 1) + mdot(high, vl[upto], 1, 1)
        )
        for j in range(g):
            gc[j, at] = gram[:, j * width : (j + 1) * width]
        w = wbuf[g]
        gdbuf[g] = gram[:, g * width :] + mm(w, w, EXACT, 1, 1)

    def factors(members):
        row_at = lax.broadcasted_iota(jnp.int32, (width, width), 0)
        col_at = lax.broadcasted_iota(jnp.int32, (width, width), 1)
        eye = (row_at == col_at).astype(jnp.float32)
        power, inverse, diag = {}, {}, {}
        for g in members:
            alive = live[:, g : g + 1]
            diag[g] = vbuf[g, :, window:] * alive + (1.0 - alive)
            first = jnp.where(col_at > row_at, -(diag[g] * gdbuf[g]), 0.0)
            inverse[g] = eye + first
            power[g] = mm(first, first, EXACT)
        reached = 2
        while reached < width:
            for g in members:
                if 2 * reached < width:
                    both = jnp.concatenate([power[g], inverse[g]], axis=0)
                    both = mm(both, power[g], EXACT)
                    power[g] = both[:width]
                    inverse[g] = inverse[g] + both[width:]
                else:
                    inverse[g] = inverse[g] + mm(inverse[g], power[g], EXACT)
            reached = reached * 2
        for g in members:
            tf = inverse[g] * diag[g].T
            w = wbuf[g]
            ew = mm(tf, w, THREE)
            e[g] = ew
            tb[g, :width] = tf
            bf = mm(w.T, jnp.concatenate([tf, ew], axis=1), THREE)
            tb[g, width:] = bf[:, :width]
            f[g] = bf[:, width:]

    pl.semaphore_wait(bar, 4)
    for g in range(3):
        c0(g)
    for j in range(groups):
        gc[j, : (j + 1) * width] = jnp.zeros(((j + 1) * width, width), jnp.float32)
    high, low = split(x[B:])
    xh[...] = high
    xl[...] = low
    c1(0)
    c1(1)
    c2(0)
    for g in range(groups):
        if g + 3 < groups:
            c0(g + 3)
        if g + 2 < groups:
            c1(g + 2)
        if g + 1 < groups:
            c2(g + 1)
        c3(g)
        c4(g)
        products(g)
        if g % 2 == 1:
            factors((g - 1, g))
    for g in range(groups):
        pltpu.make_async_copy(vbuf.at[g], vout.at[g], o_sem.at[g]).wait()
        for kind in range(9):
            sent(g, kind).wait_send()
        for mine in (True, False):
            for step in range(4):
                relay(g, mine, step).wait_send()


def prep(vin, live, x):
    groups, _, lanes = vin.shape
    row_count, columns = x.shape
    mid = row_count - B
    vm = pl.BlockSpec(memory_space=pltpu.VMEM)
    f32, b16 = jnp.float32, jnp.bfloat16
    shape = jax.ShapeDtypeStruct
    return pl.pallas_call(
        prep_kernel,
        out_shape=(
            shape((groups, B, lanes), f32),
            shape((groups, B, columns), f32),
            shape((groups, groups * B, B), f32),
            shape((groups, 3 * B, B), f32),
            shape((groups, B, 2 * B), f32),
            shape((groups, 2 * B, 2 * B), f32),
        ),
        in_specs=[vm] * 3,
        out_specs=(pl.BlockSpec(memory_space=pl.ANY),) + (vm,) * 5,
        scratch_shapes=[
            pltpu.VMEM((groups, B, lanes), f32),
            pltpu.VMEM((groups * B, mid), b16),
            pltpu.VMEM((groups * B, mid), b16),
            pltpu.VMEM((groups, B, 2 * B), f32),
            pltpu.VMEM((groups, B, B), f32),
            pltpu.VMEM((mid, columns), b16),
            pltpu.VMEM((mid, columns), b16),
            pltpu.SemaphoreType.DMA((groups, 17)),
            pltpu.SemaphoreType.DMA((groups, 17)),
            pltpu.SemaphoreType.DMA((groups,)),
        ],
        compiler_params=pltpu.CompilerParams(
            collective_id=1, has_side_effects=True, vmem_limit_bytes=56 << 20
        ),
        name="prep",
    )(vin, live, x)


def chain_kernel(
    xh, pm, gc, tb, e, f, c_out, head_out, y, ty, hin, hout, xs, own, s_up0, s_up, s_dn, r_h, r_t
):
    groups = pm.shape[0]
    width = hin.shape[-1]
    chunks = hin.shape[1]
    row = lax.axis_index("row")
    rows = lax.axis_size("row")
    first = row == 0
    last = row == rows - 1

    bar = pltpu.get_barrier_semaphore()

    @pl.when(jnp.logical_not(first))
    def _():
        pl.semaphore_signal(bar, inc=1, device_id={"row": row - 1}, device_id_type=MESH)

    @pl.when(jnp.logical_not(last))
    def _():
        pl.semaphore_signal(bar, inc=1, device_id={"row": row + 1}, device_id_type=MESH)

    @pl.when(first | last)
    def _():
        pl.semaphore_wait(bar, 1)

    @pl.when(jnp.logical_not(first | last))
    def _():
        pl.semaphore_wait(bar, 2)

    def up0(k):
        return pltpu.make_async_remote_copy(
            src_ref=xs.at[k],
            dst_ref=hin.at[0, k, pl.ds(B, B)],
            send_sem=s_up0.at[k],
            recv_sem=r_t.at[0, k],
            device_id={"row": row - 1},
            device_id_type=MESH,
        )

    def up(g, k):
        return pltpu.make_async_remote_copy(
            src_ref=hout.at[g, k, pl.ds(0, B)],
            dst_ref=hin.at[g + 1, k, pl.ds(B, B)],
            send_sem=s_up.at[g, k],
            recv_sem=r_t.at[g + 1, k],
            device_id={"row": row - 1},
            device_id_type=MESH,
        )

    def down(g, k):
        return pltpu.make_async_remote_copy(
            src_ref=hout.at[g, k, pl.ds(B, B)],
            dst_ref=hin.at[g, k, pl.ds(0, B)],
            send_sem=s_dn.at[g, k],
            recv_sem=r_h.at[g, k],
            device_id={"row": row + 1},
            device_id_type=MESH,
        )

    def recv_h(g, k):
        return pltpu.make_async_remote_copy(
            src_ref=hout.at[g, k, pl.ds(B, B)],
            dst_ref=hin.at[g, k, pl.ds(0, B)],
            send_sem=s_dn.at[g, k],
            recv_sem=r_h.at[g, k],
            device_id={"row": row - 1},
            device_id_type=MESH,
        )

    def recv_t(g, k):
        return pltpu.make_async_remote_copy(
            src_ref=xs.at[k],
            dst_ref=hin.at[g, k, pl.ds(B, B)],
            send_sem=s_up0.at[k],
            recv_sem=r_t.at[g, k],
            device_id={"row": row + 1},
            device_id_type=MESH,
        )

    for k in range(chunks):
        xs[k] = xh[:, k * width : (k + 1) * width]
        own[k] = xs[k]

    @pl.when(jnp.logical_not(first))
    def _():
        for k in range(chunks):
            up0(k).start()

    @pl.when(last)
    def _():
        for g in range(groups):
            for k in range(chunks):
                hin[g, k, B:] = jnp.zeros((B, width), jnp.float32)

    y[...] = pm[...]
    ty[...] = mm(tb[0], pm[0], THREE)

    def step(g, carry):
        for k in range(chunks):
            cols = slice(k * width, (k + 1) * width)

            @pl.when(jnp.logical_not(first))
            def _():
                recv_h(g, k).wait_recv()

            @pl.when(jnp.logical_not(last))
            def _():
                recv_t(g, k).wait_recv()

            top = jnp.where(first, own[k], hin[g, k, :B])
            h = jnp.concatenate([top, hin[g, k, B:]], axis=0)
            hn = (h - ty[B:, cols]) - mm(f[g], h, THREE)
            hout[g, k] = hn

            @pl.when(jnp.logical_not(last))
            def _():
                down(g, k).start()

            @pl.when(jnp.logical_not(first) & (g < groups - 1))
            def _():
                up(g, k).start()

            own[k] = hn[:B]
            c_out[g, :, cols] = ty[:B, cols] + mm(e[g], h, THREE)

        @pl.when(g < groups - 1)
        def _():
            change = mm(gc[g], c_out[g], THREE)
            y[...] = y[...] - change.reshape(y.shape)
            ty[...] = mm(tb[g + 1], y[g + 1], THREE)

        return carry

    lax.fori_loop(0, groups, step, 0)
    for k in range(chunks):
        head_out[:, k * width : (k + 1) * width] = hout[groups - 1, k, :B]

    @pl.when(jnp.logical_not(first))
    def _():
        for k in range(chunks):
            up0(k).wait_send()

        def drain(g, carry):
            for k in range(chunks):
                up(g, k).wait_send()
            return carry

        lax.fori_loop(0, groups - 1, drain, 0)

    @pl.when(jnp.logical_not(last))
    def _():
        def drain(g, carry):
            for k in range(chunks):
                down(g, k).wait_send()
            return carry

        lax.fori_loop(0, groups, drain, 0)


def chain(xh, pm, gc, tb, e, f):
    groups, _, columns = pm.shape
    width = columns // NC
    vm = pl.BlockSpec(memory_space=pltpu.VMEM)
    f32 = jnp.float32
    return pl.pallas_call(
        chain_kernel,
        out_shape=(
            jax.ShapeDtypeStruct((groups, B, columns), f32),
            jax.ShapeDtypeStruct((B, columns), f32),
        ),
        in_specs=[vm] * 6,
        out_specs=(vm, vm),
        scratch_shapes=[
            pltpu.VMEM((groups, B, columns), f32),
            pltpu.VMEM((3 * B, columns), f32),
            pltpu.VMEM((groups, NC, 2 * B, width), f32),
            pltpu.VMEM((groups, NC, 2 * B, width), f32),
            pltpu.VMEM((NC, B, width), f32),
            pltpu.VMEM((NC, B, width), f32),
            pltpu.SemaphoreType.DMA((NC,)),
            pltpu.SemaphoreType.DMA((groups, NC)),
            pltpu.SemaphoreType.DMA((groups, NC)),
            pltpu.SemaphoreType.DMA((groups, NC)),
            pltpu.SemaphoreType.DMA((groups, NC)),
        ],
        compiler_params=pltpu.CompilerParams(
            collective_id=0, has_side_effects=True, vmem_limit_bytes=40 << 20
        ),
        name="chain",
    )(xh, pm, gc, tb, e, f)


def per_device(x, mirror_entries, tau, tallies):
    row_count, columns = x.shape
    groups, _, own, window = mirror_entries.shape
    lane_tau = jnp.broadcast_to(tau[:, 0, :, None], (groups, own, B))
    vin = jnp.concatenate([mirror_entries[:, 0], lane_tau], axis=2)
    live = (lax.iota(jnp.int32, B)[:, None] < tallies[:, 0][None, :]).astype(jnp.float32)
    live = jnp.pad(live, ((0, 0), (0, B - groups)))
    v, pm, gc, tb, e, f = prep(vin, live, x)
    c, head = chain(x[:B], pm, gc, tb, e, f)
    mid = v.reshape(groups * B, window + B)[:, B:row_count]
    out_mid = x[B:] - mm(mid, c.reshape(groups * B, columns), THREE, 0, 0)
    return jnp.concatenate([head, out_mid], axis=0)


def solution(mesh):
    in_specs = (P("row", "col"), P(None, "row", "col", None), P(None, "row", "col"), P(None, "row"))
    return jax.shard_map(
        per_device, mesh=mesh, in_specs=in_specs, out_specs=P("row", "col"), check_vma=False
    )
```

```python
import jax
import jax.numpy as jnp
from jax import lax
from jax.experimental import pallas as pl
from jax.experimental.pallas import tpu as pltpu
from jax.sharding import PartitionSpec as P

EXACT = lax.Precision.HIGHEST
THREE = lax.Precision.HIGH
MESH = pl.DeviceIdType.MESH
B = 128
NC = 4


def mm(a, b, precision, ca=1, cb=0):
    return lax.dot_general(
        a, b, (((ca,), (cb,)), ((), ())), precision=precision, preferred_element_type=jnp.float32
    )


def mdot(a, b, ca=1, cb=0):
    return lax.dot_general(a, b, (((ca,), (cb,)), ((), ())), preferred_element_type=jnp.float32)


def split(value):
    high = value.astype(jnp.bfloat16)
    return high, (value - high.astype(jnp.float32)).astype(jnp.bfloat16)


def fused_kernel(
    vin, ltau, counts, xhbm, vh_out, vl_out, c_out, head_out, x, vbuf, vh, vl, wbuf, xh, xl, pm, grow, tb, e, f,
    ty, hin, hout, xs, own, s_sem, r_sem, o_sem, x_sem, s_up0, s_up, s_dn, r_h, r_t
):
    chunks, part = hin.shape[1], hin.shape[3]
    groups, width, lanes = vbuf.shape
    window = lanes - B
    row_count = x.shape[0]
    half = lanes // 2
    row, col = lax.axis_index("row"), lax.axis_index("col")
    rows = lax.axis_size("row")
    first, last = row == 0, row == rows - 1
    keep = (row != rows - 1).astype(jnp.float32)
    side, yy, core = col // 8, (col % 8) // 2, col % 2

    def shard(side_, y_):
        return side_ * 8 + (y_ % 4) * 2 + core

    other = 1 - side
    to_up = shard(side, yy + 1)
    to_down = shard(side, yy + 3)
    to_x = shard(other, yy)
    to_sib = col + 1 - 2 * core

    x_copy = pltpu.make_async_copy(xhbm, x, x_sem)
    x_copy.start()
    bar = pltpu.get_barrier_semaphore()
    for target in (to_up, to_down, to_x, to_sib):
        pl.semaphore_signal(bar, inc=1, device_id={"col": target}, device_id_type=MESH)

    @pl.when(jnp.logical_not(first))
    def _():
        pl.semaphore_signal(bar, inc=1, device_id={"row": row - 1}, device_id_type=MESH)

    @pl.when(jnp.logical_not(last))
    def _():
        pl.semaphore_signal(bar, inc=1, device_id={"row": row + 1}, device_id_type=MESH)

    def rows_of(owner):
        return pl.ds(pl.multiple_of(owner * 8, 8), 8)

    for g in range(groups):
        vbuf[g, rows_of(col), :window] = vin[g, 0]
        vbuf[g, rows_of(col), window:] = jnp.broadcast_to(ltau[g], (8, B))

    def copy(g, kind, owner, target, part=None):
        span = pl.ds(0, lanes) if part is None else pl.ds(part * half, half)
        place = vbuf.at[g, rows_of(owner), span]
        return pltpu.make_async_remote_copy(
            src_ref=place,
            dst_ref=place,
            send_sem=s_sem.at[g, kind],
            recv_sem=r_sem.at[g, kind],
            device_id={"col": target},
            device_id_type=MESH,
        )

    def sent(g, kind):
        owner, target, part = (
            (col, to_up, None),
            (col, to_down, None),
            (col, to_x, None),
            (shard(side, yy + 3), to_up, 0),
            (shard(side, yy + 1), to_down, 1),
            (shard(other, yy), to_up, None),
            (shard(other, yy), to_down, None),
            (shard(other, yy + 3), to_up, 0),
            (shard(other, yy + 1), to_down, 1),
        )[kind]
        return copy(g, kind, owner, target, part)

    def got(g, kind):
        owner, part = (
            (shard(side, yy + 3), None),
            (shard(side, yy + 1), None),
            (shard(other, yy), None),
            (shard(side, yy + 2), 0),
            (shard(side, yy + 2), 1),
            (shard(other, yy + 3), None),
            (shard(other, yy + 1), None),
            (shard(other, yy + 2), 0),
            (shard(other, yy + 2), 1),
        )[kind]
        return copy(g, kind, owner, to_up, part)

    def relay(g, mine, step):
        owner = shard(side if mine else other, yy + step)
        return copy(g, (9 if mine else 13) + step, owner, to_sib)

    def relayed(g, mine, step):
        owner = shard(side if mine else other, yy + step) + 1 - 2 * core
        return copy(g, (9 if mine else 13) + step, owner, to_sib)

    def c0(g):
        for kind in (0, 1, 2):
            sent(g, kind).start()
        relay(g, True, 0).start()

    def c1(g):
        got(g, 0).wait_recv()
        sent(g, 3).start()
        relay(g, True, 3).start()
        got(g, 1).wait_recv()
        sent(g, 4).start()
        relay(g, True, 1).start()
        got(g, 2).wait_recv()
        sent(g, 5).start()
        sent(g, 6).start()
        relay(g, False, 0).start()

    def c2(g):
        got(g, 5).wait_recv()
        sent(g, 7).start()
        relay(g, False, 3).start()
        got(g, 6).wait_recv()
        sent(g, 8).start()
        relay(g, False, 1).start()
        got(g, 3).wait_recv()
        got(g, 4).wait_recv()
        relay(g, True, 2).start()

    def c3(g):
        got(g, 7).wait_recv()
        got(g, 8).wait_recv()
        relay(g, False, 2).start()

    def c4(g):
        for mine in (True, False):
            for step in range(4):
                relayed(g, mine, step).wait_recv()

    def alive_of(g, size):
        at = lax.broadcasted_iota(jnp.int32, (width, size), 0)
        return (at < counts[g, 0]).astype(jnp.float32)

    def products(g):
        alive = alive_of(g, 1)
        high, low = split(vbuf[g, :, B:row_count] * alive)
        vh[g] = high
        vl[g] = low
        pltpu.make_async_copy(vh.at[g], vh_out.at[g], o_sem.at[g, 0]).start()
        pltpu.make_async_copy(vl.at[g], vl_out.at[g], o_sem.at[g, 1]).start()
        wbuf[g, :, :B] = vbuf[g, :, :B] * alive
        wbuf[g, :, B:] = vbuf[g, :, row_count:window] * (alive * keep)
        pm[g] = mdot(high, xh[...]) + mdot(low, xh[...]) + mdot(high, xl[...])

    def grams(g):
        high, low = vh[g], vl[g]
        allh = vh[...].reshape(groups * width, row_count - B)
        alll = vl[...].reshape(groups * width, row_count - B)
        grow[g] = mdot(high, allh, 1, 1) + mdot(low, allh, 1, 1) + mdot(high, alll, 1, 1)

    def factors(g):
        row_at = lax.broadcasted_iota(jnp.int32, (width, width), 0)
        col_at = lax.broadcasted_iota(jnp.int32, (width, width), 1)
        eye = (row_at == col_at).astype(jnp.float32)
        alive = alive_of(g, width)
        w = wbuf[g]
        here = pl.ds(pl.multiple_of(g * width, width), width)
        gram = grow[g, :, here] + mm(w, w, EXACT, 1, 1)
        grow[g, :, here] = jnp.zeros((width, width), jnp.float32)
        diag = vbuf[g, :, window:] * alive + (1.0 - alive)
        power = jnp.where(col_at > row_at, -(diag * gram), 0.0)
        inverse = eye + power
        power = mm(power, power, EXACT)
        reached = 2
        while reached < width:
            if 2 * reached < width:
                both = mm(jnp.concatenate([power, inverse], axis=0), power, EXACT)
                power = both[:width]
                inverse = inverse + both[width:]
            else:
                inverse = inverse + mm(inverse, power, EXACT)
            reached = reached * 2
        tf = inverse * diag.T
        ew = mm(tf, w, THREE)
        e[g] = ew
        tb[g, :width] = tf
        bf = mm(w.T, jnp.concatenate([tf, ew], axis=1), THREE)
        tb[g, width:] = bf[:, :width]
        f[g] = bf[:, width:]

    @pl.when(first | last)
    def _():
        pl.semaphore_wait(bar, 5)

    @pl.when(jnp.logical_not(first | last))
    def _():
        pl.semaphore_wait(bar, 6)

    c0(0)
    c0(1)
    vh[...] = jnp.zeros_like(vh)
    vl[...] = jnp.zeros_like(vl)
    c_out[...] = jnp.zeros_like(c_out)

    def up0(k):
        return pltpu.make_async_remote_copy(
            src_ref=xs.at[k],
            dst_ref=hin.at[0, k, pl.ds(B, B)],
            send_sem=s_up0.at[k],
            recv_sem=r_t.at[0, k],
            device_id={"row": row - 1},
            device_id_type=MESH,
        )

    def up(g, k):
        return pltpu.make_async_remote_copy(
            src_ref=hout.at[g, k, pl.ds(0, B)],
            dst_ref=hin.at[g + 1, k, pl.ds(B, B)],
            send_sem=s_up.at[g, k],
            recv_sem=r_t.at[g + 1, k],
            device_id={"row": row - 1},
            device_id_type=MESH,
        )

    def down(g, k):
        return pltpu.make_async_remote_copy(
            src_ref=hout.at[g, k, pl.ds(B, B)],
            dst_ref=hin.at[g, k, pl.ds(0, B)],
            send_sem=s_dn.at[g, k],
            recv_sem=r_h.at[g, k],
            device_id={"row": row + 1},
            device_id_type=MESH,
        )

    def recv_h(g, k):
        return pltpu.make_async_remote_copy(
            src_ref=hout.at[g, k, pl.ds(B, B)],
            dst_ref=hin.at[g, k, pl.ds(0, B)],
            send_sem=s_dn.at[g, k],
            recv_sem=r_h.at[g, k],
            device_id={"row": row - 1},
            device_id_type=MESH,
        )

    def recv_t(g, k):
        return pltpu.make_async_remote_copy(
            src_ref=xs.at[k],
            dst_ref=hin.at[g, k, pl.ds(B, B)],
            send_sem=s_up0.at[k],
            recv_sem=r_t.at[g, k],
            device_id={"row": row + 1},
            device_id_type=MESH,
        )

    x_copy.wait()
    for k in range(chunks):
        xs[k] = x[:B, k * part : (k + 1) * part]
        own[k] = xs[k]

    @pl.when(jnp.logical_not(first))
    def _():
        for k in range(chunks):
            up0(k).start()

    @pl.when(last)
    def _():
        for g in range(groups):
            for k in range(chunks):
                hin[g, k, B:] = jnp.zeros((B, part), jnp.float32)

    high, low = split(x[B:])
    xh[...] = high
    xl[...] = low
    c1(0)
    c0(2)
    c2(0)
    c1(1)
    lead = jnp.minimum(1 + row // 2, groups)

    def link(g, k):
        cols = slice(k * part, (k + 1) * part)

        @pl.when(jnp.logical_not(first))
        def _():
            recv_h(g, k).wait_recv()

        @pl.when(jnp.logical_not(last))
        def _():
            recv_t(g, k).wait_recv()

        top = jnp.where(first, own[k], hin[g, k, :B])
        h = jnp.concatenate([top, hin[g, k, B:]], axis=0)
        hn = (h - ty[B:, cols]) - mm(f[g], h, THREE)
        hout[g, k] = hn

        @pl.when(jnp.logical_not(last))
        def _():
            down(g, k).start()

        @pl.when(jnp.logical_not(first) & (g < groups - 1))
        def _():
            up(g, k).start()

        own[k] = hn[:B]
        c_out[g, :, cols] = ty[:B, cols] + mm(e[g], h, THREE)

    def step(t, carry):
        @pl.when(t < groups)
        def _():
            c3(t)

        @pl.when(t + 3 < groups)
        def _():
            c0(t + 3)

        @pl.when(t + 1 < groups)
        def _():
            c2(t + 1)

        @pl.when(t + 2 < groups)
        def _():
            c1(t + 2)

        def chain(k):
            @pl.when((t >= lead) & (t < lead + groups))
            def _():
                link(t - lead, k)

        def work(piece):
            @pl.when(t < groups)
            def _():
                piece(t)

        chain(0)
        work(c4)
        work(products)
        chain(1)
        work(grams)
        chain(2)
        work(factors)
        chain(3)

        @pl.when((t >= lead - 1) & (t < lead + groups - 1))
        def _():
            g = t - lead + 1
            whole = c_out[...].reshape(groups * width, c_out.shape[2])
            ty[...] = mm(tb[g], pm[g] - mm(grow[g], whole, THREE), THREE)

        return carry

    lax.fori_loop(0, lead + groups, step, 0)
    for k in range(chunks):
        head_out[:, k * part : (k + 1) * part] = hout[groups - 1, k, :B]

    @pl.when(jnp.logical_not(first))
    def _():
        for k in range(chunks):
            up0(k).wait_send()

        def drain(g, carry):
            for k in range(chunks):
                up(g, k).wait_send()
            return carry

        lax.fori_loop(0, groups - 1, drain, 0)

    @pl.when(jnp.logical_not(last))
    def _():
        def drain(g, carry):
            for k in range(chunks):
                down(g, k).wait_send()
            return carry

        lax.fori_loop(0, groups, drain, 0)

    for g in range(groups):
        pltpu.make_async_copy(vh.at[g], vh_out.at[g], o_sem.at[g, 0]).wait()
        pltpu.make_async_copy(vl.at[g], vl_out.at[g], o_sem.at[g, 1]).wait()
        for kind in range(9):
            sent(g, kind).wait_send()
        for mine in (True, False):
            for step in range(4):
                relay(g, mine, step).wait_send()


def fused(vin, ltau, live, x):
    groups, _, own, window = vin.shape
    lanes = window + B
    row_count, columns = x.shape
    mid = row_count - B
    part = columns // NC
    vm = pl.BlockSpec(memory_space=pltpu.VMEM)
    anywhere = pl.BlockSpec(memory_space=pl.ANY)
    f32, b16 = jnp.float32, jnp.bfloat16
    shape = jax.ShapeDtypeStruct
    dma = pltpu.SemaphoreType.DMA
    return pl.pallas_call(
        fused_kernel,
        out_shape=(
            shape((groups, B, mid), b16),
            shape((groups, B, mid), b16),
            shape((groups, B, columns), f32),
            shape((B, columns), f32),
        ),
        in_specs=[vm, vm, pl.BlockSpec(memory_space=pltpu.SMEM), anywhere],
        out_specs=(anywhere, anywhere, vm, vm),
        scratch_shapes=[
            pltpu.VMEM((row_count, columns), f32),
            pltpu.VMEM((groups, B, lanes), f32),
            pltpu.VMEM((groups, B, mid), b16),
            pltpu.VMEM((groups, B, mid), b16),
            pltpu.VMEM((groups, B, 2 * B), f32),
            pltpu.VMEM((mid, columns), b16),
            pltpu.VMEM((mid, columns), b16),
            pltpu.VMEM((groups, B, columns), f32),
            pltpu.VMEM((groups, B, groups * B), f32),
            pltpu.VMEM((groups, 3 * B, B), f32),
            pltpu.VMEM((groups, B, 2 * B), f32),
            pltpu.VMEM((groups, 2 * B, 2 * B), f32),
            pltpu.VMEM((3 * B, columns), f32),
            pltpu.VMEM((groups, NC, 2 * B, part), f32),
            pltpu.VMEM((groups, NC, 2 * B, part), f32),
            pltpu.VMEM((NC, B, part), f32),
            pltpu.VMEM((NC, B, part), f32),
            dma((groups, 17)),
            dma((groups, 17)),
            dma((groups, 2)),
            dma,
            dma((NC,)),
            dma((groups, NC)),
            dma((groups, NC)),
            dma((groups, NC)),
            dma((groups, NC)),
        ],
        compiler_params=pltpu.CompilerParams(
            collective_id=0, has_side_effects=True, vmem_limit_bytes=60 << 20
        ),
        name="fused",
    )(vin, ltau, live, x)


def finish_kernel(vh_hbm, vl_hbm, c, head, x_hbm, out, x, vh, vl, ch, cl, sem, o_sem):
    pieces, size = x.shape[0], x.shape[1]
    groups, width, _ = vh.shape

    def loads(i):
        cols = pl.ds(i * size, size)
        return (
            pltpu.make_async_copy(x_hbm.at[pl.ds(B + i * size, size)], x.at[i], sem.at[i, 0]),
            pltpu.make_async_copy(vh_hbm.at[:, :, cols], vh.at[:, :, cols], sem.at[i, 1]),
            pltpu.make_async_copy(vl_hbm.at[:, :, cols], vl.at[:, :, cols], sem.at[i, 2]),
        )

    def store(i):
        return pltpu.make_async_copy(x.at[i], out.at[pl.ds(B + i * size, size)], o_sem.at[i])

    for i in range(pieces):
        for load in loads(i):
            load.start()
    top = pltpu.make_async_copy(head, out.at[pl.ds(0, B)], o_sem.at[pieces])
    top.start()
    high, low = split(c[...].reshape(ch.shape))
    ch[...] = high
    cl[...] = low
    for i in range(pieces):
        for load in loads(i):
            load.wait()
        cols = slice(i * size, (i + 1) * size)
        high = vh[:, :, cols].reshape(groups * width, size)
        low = vl[:, :, cols].reshape(groups * width, size)
        change = mdot(high, ch[...], 0, 0) + mdot(low, ch[...], 0, 0) + mdot(high, cl[...], 0, 0)
        x[i] = x[i] - change
        store(i).start()
    top.wait()
    for i in range(pieces):
        store(i).wait()


def finish(vh, vl, c, head, x):
    groups, width, mid = vh.shape
    pieces = 5
    size = mid // pieces
    columns = x.shape[1]
    vm = pl.BlockSpec(memory_space=pltpu.VMEM)
    anywhere = pl.BlockSpec(memory_space=pl.ANY)
    dma = pltpu.SemaphoreType.DMA
    return pl.pallas_call(
        finish_kernel,
        out_shape=jax.ShapeDtypeStruct(x.shape, x.dtype),
        in_specs=[anywhere, anywhere, vm, vm, anywhere],
        out_specs=anywhere,
        scratch_shapes=[
            pltpu.VMEM((pieces, size, columns), jnp.float32),
            pltpu.VMEM(vh.shape, jnp.bfloat16),
            pltpu.VMEM(vh.shape, jnp.bfloat16),
            pltpu.VMEM((groups * width, columns), jnp.bfloat16),
            pltpu.VMEM((groups * width, columns), jnp.bfloat16),
            dma((pieces, 3)),
            dma((pieces + 1,)),
        ],
        compiler_params=pltpu.CompilerParams(vmem_limit_bytes=56 << 20),
        name="finish",
    )(vh, vl, c, head, x)


def per_device(x, mirror_entries, tau, tallies):
    vh, vl, c, head = fused(mirror_entries, tau[:, 0, :, None], tallies, x)
    return finish(vh, vl, c, head, x)


def solution(mesh):
    in_specs = (P("row", "col"), P(None, "row", "col", None), P(None, "row", "col"), P(None, "row"))
    return jax.shard_map(
        per_device, mesh=mesh, in_specs=in_specs, out_specs=P("row", "col"), check_vma=False
    )
```

```python
import jax
import jax.numpy as jnp
from jax import lax
from jax.experimental import pallas as pl
from jax.experimental.pallas import tpu as pltpu
from jax.sharding import PartitionSpec as P

EXACT = lax.Precision.HIGHEST
THREE = lax.Precision.HIGH
MESH = pl.DeviceIdType.MESH
B = 128
NC = 4


def mm(a, b, precision, ca=1, cb=0):
    return lax.dot_general(
        a, b, (((ca,), (cb,)), ((), ())), precision=precision, preferred_element_type=jnp.float32
    )


def mdot(a, b, ca=1, cb=0):
    return lax.dot_general(a, b, (((ca,), (cb,)), ((), ())), preferred_element_type=jnp.float32)


def split(value):
    high = value.astype(jnp.bfloat16)
    return high, (value - high.astype(jnp.float32)).astype(jnp.bfloat16)


def fused_kernel(
    vin, ltau, counts, xhbm, x_out, vh_out, vl_out, c_out, head_out, x, cc, vbuf, vh, vl, wbuf, xh, xl, pm, grow, tb, e, f,
    ty, hin, hout, xs, own, s_sem, r_sem, o_sem, x_sem, xo_sem, s_up0, s_up, s_dn, r_h, r_t
):
    chunks, part = hin.shape[1], hin.shape[3]
    groups, width, lanes = vbuf.shape
    window = lanes - B
    row_count = x.shape[0]
    half = lanes // 2
    row, col = lax.axis_index("row"), lax.axis_index("col")
    rows = lax.axis_size("row")
    first, last = row == 0, row == rows - 1
    keep = (row != rows - 1).astype(jnp.float32)
    side, yy, core = col // 8, (col % 8) // 2, col % 2

    def shard(side_, y_):
        return side_ * 8 + (y_ % 4) * 2 + core

    other = 1 - side
    to_up = shard(side, yy + 1)
    to_down = shard(side, yy + 3)
    to_x = shard(other, yy)
    to_sib = col + 1 - 2 * core

    x_copy = pltpu.make_async_copy(xhbm, x, x_sem)
    x_copy.start()
    bar = pltpu.get_barrier_semaphore()
    for target in (to_up, to_down, to_x, to_sib):
        pl.semaphore_signal(bar, inc=1, device_id={"col": target}, device_id_type=MESH)

    @pl.when(jnp.logical_not(first))
    def _():
        pl.semaphore_signal(bar, inc=1, device_id={"row": row - 1}, device_id_type=MESH)

    @pl.when(jnp.logical_not(last))
    def _():
        pl.semaphore_signal(bar, inc=1, device_id={"row": row + 1}, device_id_type=MESH)

    def rows_of(owner):
        return pl.ds(pl.multiple_of(owner * 8, 8), 8)

    eighth = lax.broadcasted_iota(jnp.int32, (8, B), 0)
    for g in range(groups):
        vbuf[g, rows_of(col), :window] = vin[g, 0]
        scale = jnp.zeros((8, B), jnp.float32)
        for i in range(8):
            scale = jnp.where(eighth == i, ltau[g, 0, i], scale)
        vbuf[g, rows_of(col), window:] = scale

    def copy(g, kind, owner, target, part=None):
        span = pl.ds(0, lanes) if part is None else pl.ds(part * half, half)
        place = vbuf.at[g, rows_of(owner), span]
        return pltpu.make_async_remote_copy(
            src_ref=place,
            dst_ref=place,
            send_sem=s_sem.at[g, kind],
            recv_sem=r_sem.at[g, kind],
            device_id={"col": target},
            device_id_type=MESH,
        )

    def sent(g, kind):
        owner, target, part = (
            (col, to_up, None),
            (col, to_down, None),
            (col, to_x, None),
            (shard(side, yy + 3), to_up, 0),
            (shard(side, yy + 1), to_down, 1),
            (shard(other, yy), to_up, None),
            (shard(other, yy), to_down, None),
            (shard(other, yy + 3), to_up, 0),
            (shard(other, yy + 1), to_down, 1),
        )[kind]
        return copy(g, kind, owner, target, part)

    def got(g, kind):
        owner, part = (
            (shard(side, yy + 3), None),
            (shard(side, yy + 1), None),
            (shard(other, yy), None),
            (shard(side, yy + 2), 0),
            (shard(side, yy + 2), 1),
            (shard(other, yy + 3), None),
            (shard(other, yy + 1), None),
            (shard(other, yy + 2), 0),
            (shard(other, yy + 2), 1),
        )[kind]
        return copy(g, kind, owner, to_up, part)

    def relay(g, mine, step):
        owner = shard(side if mine else other, yy + step)
        return copy(g, (9 if mine else 13) + step, owner, to_sib)

    def relayed(g, mine, step):
        owner = shard(side if mine else other, yy + step) + 1 - 2 * core
        return copy(g, (9 if mine else 13) + step, owner, to_sib)

    def c0(g):
        for kind in (0, 1):
            sent(g, kind).start()
        relay(g, True, 0).start()

    def c1(g):
        got(g, 0).wait_recv()
        sent(g, 3).start()
        relay(g, True, 3).start()
        got(g, 1).wait_recv()
        sent(g, 4).start()
        relay(g, True, 1).start()
        got(g, 2).wait_recv()
        sent(g, 5).start()
        sent(g, 6).start()
        relay(g, False, 0).start()

    def c2(g):
        got(g, 5).wait_recv()
        sent(g, 7).start()
        relay(g, False, 3).start()
        got(g, 6).wait_recv()
        sent(g, 8).start()
        relay(g, False, 1).start()
        got(g, 3).wait_recv()
        got(g, 4).wait_recv()
        relay(g, True, 2).start()

    def c3(g):
        got(g, 7).wait_recv()
        got(g, 8).wait_recv()
        relay(g, False, 2).start()

    def c4(g):
        for mine in (True, False):
            for step in range(4):
                relayed(g, mine, step).wait_recv()

    def alive_of(g, size):
        at = lax.broadcasted_iota(jnp.int32, (width, size), 0)
        return (at < counts[g]).astype(jnp.float32)

    def products(g):
        alive = alive_of(g, 1)
        high, low = split(vbuf[g, :, B:row_count] * alive)
        vh[g] = high
        vl[g] = low
        wbuf[g, :, :B] = vbuf[g, :, :B] * alive
        wbuf[g, :, B:] = vbuf[g, :, row_count:window] * (alive * keep)
        pm[g] = mdot(high, xh[...]) + mdot(low, xh[...]) + mdot(high, xl[...])

    def grams(g):
        def against(count):
            high, low = vh[g], vl[g]
            allh = vh[:count].reshape(count * width, row_count - B)
            alll = vl[:count].reshape(count * width, row_count - B)
            grow[g, :, : count * width] = (
                mdot(high, allh, 1, 1) + mdot(low, allh, 1, 1) + mdot(high, alll, 1, 1)
            )

        for low_g, high_g in ((0, 1), (1, groups // 2), (groups // 2, groups)):

            @pl.when((g >= low_g) & (g < high_g))
            def _():
                against(high_g)

    def factors(g):
        row_at = lax.broadcasted_iota(jnp.int32, (width, width), 0)
        col_at = lax.broadcasted_iota(jnp.int32, (width, width), 1)
        eye = (row_at == col_at).astype(jnp.float32)
        alive = alive_of(g, width)
        w = wbuf[g]
        here = pl.ds(pl.multiple_of(g * width, width), width)
        gram = grow[g, :, here] + mm(w, w, EXACT, 1, 1)
        grow[g, :, here] = jnp.zeros((width, width), jnp.float32)
        diag = vbuf[g, :, window:] * alive + (1.0 - alive)
        power = jnp.where(col_at > row_at, -(diag * gram), 0.0)
        inverse = eye + power
        power = mm(power, power, EXACT)
        reached = 2
        while reached < width:
            if 2 * reached < width:
                both = mm(jnp.concatenate([power, inverse], axis=0), power, EXACT)
                power = both[:width]
                inverse = inverse + both[width:]
            else:
                inverse = inverse + mm(inverse, power, EXACT)
            reached = reached * 2
        tf = inverse * diag.T
        ew = mm(tf, w, THREE)
        e[g] = ew
        tb[g, :width] = tf
        bf = mm(w.T, jnp.concatenate([tf, ew], axis=1), THREE)
        tb[g, width:] = bf[:, :width]
        f[g] = bf[:, width:]

    @pl.when(first | last)
    def _():
        pl.semaphore_wait(bar, 5)

    @pl.when(jnp.logical_not(first | last))
    def _():
        pl.semaphore_wait(bar, 6)

    sent(0, 2).start()
    c0(0)
    sent(1, 2).start()
    c0(1)
    vh[...] = jnp.zeros_like(vh)
    vl[...] = jnp.zeros_like(vl)
    cc[...] = jnp.zeros_like(cc)
    grow[...] = jnp.zeros_like(grow)

    def up0(k):
        return pltpu.make_async_remote_copy(
            src_ref=xs.at[k],
            dst_ref=hin.at[0, k, pl.ds(B, B)],
            send_sem=s_up0.at[k],
            recv_sem=r_t.at[0, k],
            device_id={"row": row - 1},
            device_id_type=MESH,
        )

    def up(g, k):
        return pltpu.make_async_remote_copy(
            src_ref=hout.at[g, k, pl.ds(0, B)],
            dst_ref=hin.at[g + 1, k, pl.ds(B, B)],
            send_sem=s_up.at[g, k],
            recv_sem=r_t.at[g + 1, k],
            device_id={"row": row - 1},
            device_id_type=MESH,
        )

    def down(g, k):
        return pltpu.make_async_remote_copy(
            src_ref=hout.at[g, k, pl.ds(B, B)],
            dst_ref=hin.at[g, k, pl.ds(0, B)],
            send_sem=s_dn.at[g, k],
            recv_sem=r_h.at[g, k],
            device_id={"row": row + 1},
            device_id_type=MESH,
        )

    def recv_h(g, k):
        return pltpu.make_async_remote_copy(
            src_ref=hout.at[g, k, pl.ds(B, B)],
            dst_ref=hin.at[g, k, pl.ds(0, B)],
            send_sem=s_dn.at[g, k],
            recv_sem=r_h.at[g, k],
            device_id={"row": row - 1},
            device_id_type=MESH,
        )

    def recv_t(g, k):
        return pltpu.make_async_remote_copy(
            src_ref=xs.at[k],
            dst_ref=hin.at[g, k, pl.ds(B, B)],
            send_sem=s_up0.at[k],
            recv_sem=r_t.at[g, k],
            device_id={"row": row + 1},
            device_id_type=MESH,
        )

    x_copy.wait()
    for k in range(chunks):
        xs[k] = x[:B, k * part : (k + 1) * part]
        own[k] = xs[k]

    @pl.when(jnp.logical_not(first))
    def _():
        for k in range(chunks):
            up0(k).start()

    for g in range(2, groups):
        sent(g, 2).start()

    @pl.when(last)
    def _():
        for g in range(groups):
            for k in range(chunks):
                hin[g, k, B:] = jnp.zeros((B, part), jnp.float32)

    high, low = split(x[B:])
    xh[...] = high
    xl[...] = low
    c1(0)
    c0(2)
    c2(0)
    c1(1)
    x_back = pltpu.make_async_copy(x, x_out, xo_sem)
    v_back = (
        pltpu.make_async_copy(vh.at[groups - 1], vh_out, o_sem.at[0]),
        pltpu.make_async_copy(vl.at[groups - 1], vl_out, o_sem.at[1]),
    )
    lead = jnp.minimum(1 + row // 2, groups)

    def link(g, k):
        cols = slice(k * part, (k + 1) * part)

        @pl.when(jnp.logical_not(first))
        def _():
            recv_h(g, k).wait_recv()

        @pl.when(jnp.logical_not(last))
        def _():
            recv_t(g, k).wait_recv()

        top = jnp.where(first, own[k], hin[g, k, :B])
        h = jnp.concatenate([top, hin[g, k, B:]], axis=0)
        hn = (h - ty[B:, cols]) - mm(f[g], h, THREE)
        hout[g, k] = hn

        @pl.when(jnp.logical_not(last))
        def _():
            down(g, k).start()

        @pl.when(jnp.logical_not(first) & (g < groups - 1))
        def _():
            up(g, k).start()

        own[k] = hn[:B]
        cc[g, :, cols] = ty[:B, cols] + mm(e[g], h, THREE)

    def update(g, piece):
        size = (row_count - B) // 5
        high, low = split(cc[g])
        at = slice(piece * size, (piece + 1) * size)
        change = (
            mdot(vh[g, :, at], high, 0, 0)
            + mdot(vl[g, :, at], high, 0, 0)
            + mdot(vh[g, :, at], low, 0, 0)
        )
        there = slice(B + piece * size, B + (piece + 1) * size)
        x[there] = x[there] - change

    def step(t, carry):
        def comm(move, g):
            @pl.when(g < groups)
            def _():
                move(g)

        comm(c3, t)
        comm(c0, t + 3)
        comm(c2, t + 1)
        comm(c1, t + 2)

        def chain(k):
            @pl.when((t >= lead) & (t < lead + groups))
            def _():
                link(t - lead, k)

        def work(piece):
            @pl.when(t < groups)
            def _():
                piece(t)

        def spread(*pieces):
            @pl.when((t > lead) & (t < lead + groups) & ((t >= groups) | (lead == 4)))
            def _():
                for piece in pieces:
                    update(t - lead - 1, piece)

        chain(0)
        work(c4)
        work(products)
        spread(0, 1)
        chain(1)
        work(grams)
        spread(2, 3)
        chain(2)
        spread(4)

        @pl.when(t == lead + groups - 1)
        def _():
            for back in v_back:
                back.start()

        @pl.when((t == lead + groups - 1) & (lead == 4))
        def _():
            x_back.start()

        work(factors)
        chain(3)

        @pl.when((t >= lead - 1) & (t < lead + groups - 1))
        def _():
            g = t - lead + 1
            whole = cc[...].reshape(groups * width, cc.shape[2])
            ty[...] = mm(tb[g], pm[g] - mm(grow[g], whole, THREE), THREE)

        return carry

    lax.fori_loop(0, lead + groups, step, 0)

    @pl.when(lead < 4)
    def _():
        def later(g, carry):
            for piece in range(5):
                update(g, piece)
            return carry

        lax.fori_loop(0, groups - 1 - lead, later, 0)
        x_back.start()

    c_out[...] = cc[groups - 1]
    for k in range(chunks):
        head_out[:, k * part : (k + 1) * part] = hout[groups - 1, k, :B]

    @pl.when(jnp.logical_not(first))
    def _():
        for k in range(chunks):
            up0(k).wait_send()

        def drain(g, carry):
            for k in range(chunks):
                up(g, k).wait_send()
            return carry

        lax.fori_loop(0, groups - 1, drain, 0)

    @pl.when(jnp.logical_not(last))
    def _():
        def drain(g, carry):
            for k in range(chunks):
                down(g, k).wait_send()
            return carry

        lax.fori_loop(0, groups, drain, 0)

    x_back.wait()
    for back in v_back:
        back.wait()
    for g in range(groups):
        for kind in range(9):
            sent(g, kind).wait_send()
        for mine in (True, False):
            for step in range(4):
                relay(g, mine, step).wait_send()


def fused(vin, ltau, live, x):
    groups, _, own, window = vin.shape
    lanes = window + B
    row_count, columns = x.shape
    mid = row_count - B
    part = columns // NC
    vm = pl.BlockSpec(memory_space=pltpu.VMEM)
    anywhere = pl.BlockSpec(memory_space=pl.ANY)
    small = pl.BlockSpec(memory_space=pltpu.SMEM)
    f32, b16 = jnp.float32, jnp.bfloat16
    shape = jax.ShapeDtypeStruct
    dma = pltpu.SemaphoreType.DMA
    return pl.pallas_call(
        fused_kernel,
        out_shape=(
            shape((row_count, columns), f32),
            shape((B, mid), b16),
            shape((B, mid), b16),
            shape((B, columns), f32),
            shape((B, columns), f32),
        ),
        in_specs=[vm, small, small, anywhere],
        out_specs=(anywhere, anywhere, anywhere, vm, vm),
        scratch_shapes=[
            pltpu.VMEM((row_count, columns), f32),
            pltpu.VMEM((groups, B, columns), f32),
            pltpu.VMEM((groups, B, lanes), f32),
            pltpu.VMEM((groups, B, mid), b16),
            pltpu.VMEM((groups, B, mid), b16),
            pltpu.VMEM((groups, B, 2 * B), f32),
            pltpu.VMEM((mid, columns), b16),
            pltpu.VMEM((mid, columns), b16),
            pltpu.VMEM((groups, B, columns), f32),
            pltpu.VMEM((groups, B, groups * B), f32),
            pltpu.VMEM((groups, 3 * B, B), f32),
            pltpu.VMEM((groups, B, 2 * B), f32),
            pltpu.VMEM((groups, 2 * B, 2 * B), f32),
            pltpu.VMEM((3 * B, columns), f32),
            pltpu.VMEM((groups, NC, 2 * B, part), f32),
            pltpu.VMEM((groups, NC, 2 * B, part), f32),
            pltpu.VMEM((NC, B, part), f32),
            pltpu.VMEM((NC, B, part), f32),
            dma((groups, 17)),
            dma((groups, 17)),
            dma((2,)),
            dma,
            dma,
            dma((NC,)),
            dma((groups, NC)),
            dma((groups, NC)),
            dma((groups, NC)),
            dma((groups, NC)),
        ],
        compiler_params=pltpu.CompilerParams(
            collective_id=0, has_side_effects=True, vmem_limit_bytes=60 << 20
        ),
        name="fused",
    )(vin, ltau, live, x)


def finish_kernel(vh_hbm, vl_hbm, c, head, x_hbm, out, x, vh, vl, ch, cl, sem, o_sem):
    pieces, size = x.shape[0], x.shape[1]

    def loads(i):
        cols = pl.ds(i * size, size)
        return (
            pltpu.make_async_copy(x_hbm.at[pl.ds(B + i * size, size)], x.at[i], sem.at[i, 0]),
            pltpu.make_async_copy(vh_hbm.at[:, cols], vh.at[:, cols], sem.at[i, 1]),
            pltpu.make_async_copy(vl_hbm.at[:, cols], vl.at[:, cols], sem.at[i, 2]),
        )

    def store(i):
        return pltpu.make_async_copy(x.at[i], out.at[pl.ds(B + i * size, size)], o_sem.at[i])

    for i in range(pieces):
        for load in loads(i):
            load.start()
    top = pltpu.make_async_copy(head, out.at[pl.ds(0, B)], o_sem.at[pieces])
    top.start()
    high, low = split(c[...])
    ch[...] = high
    cl[...] = low
    for i in range(pieces):
        for load in loads(i):
            load.wait()
        cols = slice(i * size, (i + 1) * size)
        high = vh[:, cols]
        low = vl[:, cols]
        change = mdot(high, ch[...], 0, 0) + mdot(low, ch[...], 0, 0) + mdot(high, cl[...], 0, 0)
        x[i] = x[i] - change
        store(i).start()
    top.wait()
    for i in range(pieces):
        store(i).wait()


def finish(vh, vl, c, head, x):
    width, mid = vh.shape
    pieces = 5
    size = mid // pieces
    columns = x.shape[1]
    vm = pl.BlockSpec(memory_space=pltpu.VMEM)
    anywhere = pl.BlockSpec(memory_space=pl.ANY)
    dma = pltpu.SemaphoreType.DMA
    return pl.pallas_call(
        finish_kernel,
        out_shape=jax.ShapeDtypeStruct(x.shape, x.dtype),
        in_specs=[anywhere, anywhere, vm, vm, anywhere],
        out_specs=anywhere,
        scratch_shapes=[
            pltpu.VMEM((pieces, size, columns), jnp.float32),
            pltpu.VMEM(vh.shape, jnp.bfloat16),
            pltpu.VMEM(vh.shape, jnp.bfloat16),
            pltpu.VMEM((width, columns), jnp.bfloat16),
            pltpu.VMEM((width, columns), jnp.bfloat16),
            dma((pieces, 3)),
            dma((pieces + 1,)),
        ],
        compiler_params=pltpu.CompilerParams(vmem_limit_bytes=56 << 20),
        name="finish",
    )(vh, vl, c, head, x)


def per_device(x, mirror_entries, tau, tallies):
    rest, vh, vl, c, head = fused(mirror_entries, tau, tallies[:, 0], x)
    return finish(vh, vl, c, head, rest)


def solution(mesh):
    in_specs = (P("row", "col"), P(None, "row", "col", None), P(None, "row", "col"), P(None, "row"))
    return jax.shard_map(
        per_device, mesh=mesh, in_specs=in_specs, out_specs=P("row", "col"), check_vma=False
    )
```

```python
import jax
import jax.numpy as jnp
from jax import lax
from jax.experimental import pallas as pl
from jax.experimental.pallas import tpu as pltpu
from jax.sharding import PartitionSpec as P

EXACT = lax.Precision.HIGHEST
THREE = lax.Precision.HIGH
MESH = pl.DeviceIdType.MESH
B = 128
NC = 4


def mm(a, b, precision, ca=1, cb=0):
    return lax.dot_general(
        a, b, (((ca,), (cb,)), ((), ())), precision=precision, preferred_element_type=jnp.float32
    )


def mdot(a, b, ca=1, cb=0):
    return lax.dot_general(a, b, (((ca,), (cb,)), ((), ())), preferred_element_type=jnp.float32)


def split(value):
    high = value.astype(jnp.bfloat16)
    return high, (value - high.astype(jnp.float32)).astype(jnp.bfloat16)


def fused_kernel(
    vin, ltau, counts, xhbm, x_out, vh_out, vl_out, c_out, head_out, x, cc, vbuf, vh, vl, wbuf, xh, xl, pm, grow, tb, e, f,
    ty, hin, hout, xs, own, s_sem, r_sem, o_sem, x_sem, xo_sem, s_up0, s_up, s_dn, r_h, r_t
):
    chunks, part = hin.shape[1], hin.shape[3]
    groups, width, lanes = vbuf.shape
    window = lanes - B
    row_count = x.shape[0]
    half = lanes // 2
    row, col = lax.axis_index("row"), lax.axis_index("col")
    rows = lax.axis_size("row")
    first, last = row == 0, row == rows - 1
    keep = (row != rows - 1).astype(jnp.float32)
    side, yy, core = col // 8, (col % 8) // 2, col % 2

    def shard(side_, y_):
        return side_ * 8 + (y_ % 4) * 2 + core

    other = 1 - side
    to_up = shard(side, yy + 1)
    to_down = shard(side, yy + 3)
    to_x = shard(other, yy)
    to_sib = col + 1 - 2 * core

    x_copy = pltpu.make_async_copy(xhbm, x, x_sem)
    x_copy.start()
    bar = pltpu.get_barrier_semaphore()
    for target in (to_up, to_down, to_x, to_sib):
        pl.semaphore_signal(bar, inc=1, device_id={"col": target}, device_id_type=MESH)

    @pl.when(jnp.logical_not(first))
    def _():
        pl.semaphore_signal(bar, inc=1, device_id={"row": row - 1}, device_id_type=MESH)

    @pl.when(jnp.logical_not(last))
    def _():
        pl.semaphore_signal(bar, inc=1, device_id={"row": row + 1}, device_id_type=MESH)

    def rows_of(owner):
        return pl.ds(pl.multiple_of(owner * 8, 8), 8)

    eighth = lax.broadcasted_iota(jnp.int32, (8, B), 0)
    for g in range(groups):
        vbuf[g, rows_of(col), :window] = vin[g, 0]
        scale = jnp.zeros((8, B), jnp.float32)
        for i in range(8):
            scale = jnp.where(eighth == i, ltau[g, 0, i], scale)
        vbuf[g, rows_of(col), window:] = scale

    def copy(g, kind, owner, target, part=None):
        span = pl.ds(0, lanes) if part is None else pl.ds(part * half, half)
        place = vbuf.at[g, rows_of(owner), span]
        return pltpu.make_async_remote_copy(
            src_ref=place,
            dst_ref=place,
            send_sem=s_sem.at[g, kind],
            recv_sem=r_sem.at[g, kind],
            device_id={"col": target},
            device_id_type=MESH,
        )

    def sent(g, kind):
        owner, target, part = (
            (col, to_up, None),
            (col, to_down, None),
            (col, to_x, None),
            (shard(side, yy + 3), to_up, 0),
            (shard(side, yy + 1), to_down, 1),
            (shard(other, yy), to_up, None),
            (shard(other, yy), to_down, None),
            (shard(other, yy + 3), to_up, 0),
            (shard(other, yy + 1), to_down, 1),
        )[kind]
        return copy(g, kind, owner, target, part)

    def got(g, kind):
        owner, part = (
            (shard(side, yy + 3), None),
            (shard(side, yy + 1), None),
            (shard(other, yy), None),
            (shard(side, yy + 2), 0),
            (shard(side, yy + 2), 1),
            (shard(other, yy + 3), None),
            (shard(other, yy + 1), None),
            (shard(other, yy + 2), 0),
            (shard(other, yy + 2), 1),
        )[kind]
        return copy(g, kind, owner, to_up, part)

    def relay(g, mine, step):
        owner = shard(side if mine else other, yy + step)
        return copy(g, (9 if mine else 13) + step, owner, to_sib)

    def relayed(g, mine, step):
        owner = shard(side if mine else other, yy + step) + 1 - 2 * core
        return copy(g, (9 if mine else 13) + step, owner, to_sib)

    def c0(g):
        for kind in (0, 1):
            sent(g, kind).start()
        relay(g, True, 0).start()

    def c1(g):
        got(g, 0).wait_recv()
        sent(g, 3).start()
        relay(g, True, 3).start()
        got(g, 1).wait_recv()
        sent(g, 4).start()
        relay(g, True, 1).start()
        got(g, 2).wait_recv()
        sent(g, 5).start()
        sent(g, 6).start()
        relay(g, False, 0).start()

    def c2(g):
        got(g, 5).wait_recv()
        sent(g, 7).start()
        relay(g, False, 3).start()
        got(g, 6).wait_recv()
        sent(g, 8).start()
        relay(g, False, 1).start()
        got(g, 3).wait_recv()
        got(g, 4).wait_recv()
        relay(g, True, 2).start()

    def c3(g):
        got(g, 7).wait_recv()
        got(g, 8).wait_recv()
        relay(g, False, 2).start()

    def c4(g):
        for mine in (True, False):
            for step in range(4):
                relayed(g, mine, step).wait_recv()

    def alive_of(g, size):
        at = lax.broadcasted_iota(jnp.int32, (width, size), 0)
        return (at < counts[g]).astype(jnp.float32)

    def products(g):
        alive = alive_of(g, 1)
        high, low = split(vbuf[g, :, B:row_count] * alive)
        vh[g] = high
        vl[g] = low
        wbuf[g, :, :B] = vbuf[g, :, :B] * alive
        wbuf[g, :, B:] = vbuf[g, :, row_count:window] * (alive * keep)
        pm[g] = mdot(high, xh[...]) + mdot(low, xh[...]) + mdot(high, xl[...])

    def grams(g):
        def against(count):
            high, low = vh[g], vl[g]
            allh = vh[:count].reshape(count * width, row_count - B)
            alll = vl[:count].reshape(count * width, row_count - B)
            grow[g, :, : count * width] = (
                mdot(high, allh, 1, 1) + mdot(low, allh, 1, 1) + mdot(high, alll, 1, 1)
            )

        for low_g, high_g in ((0, 1), (1, groups // 2), (groups // 2, groups)):

            @pl.when((g >= low_g) & (g < high_g))
            def _():
                against(high_g)

    def factors(g):
        row_at = lax.broadcasted_iota(jnp.int32, (width, width), 0)
        col_at = lax.broadcasted_iota(jnp.int32, (width, width), 1)
        eye = (row_at == col_at).astype(jnp.float32)
        alive = alive_of(g, width)
        w = wbuf[g]
        here = pl.ds(pl.multiple_of(g * width, width), width)
        gram = grow[g, :, here] + mm(w, w, EXACT, 1, 1)
        grow[g, :, here] = jnp.zeros((width, width), jnp.float32)
        diag = vbuf[g, :, window:] * alive + (1.0 - alive)
        power = jnp.where(col_at > row_at, -(diag * gram), 0.0)
        inverse = eye + power
        power = mm(power, power, THREE)
        reached = 2
        while reached < width:
            if 2 * reached < width:
                both = mm(jnp.concatenate([power, inverse], axis=0), power, THREE)
                power = both[:width]
                inverse = inverse + both[width:]
            else:
                inverse = inverse + mm(inverse, power, THREE)
            reached = reached * 2
        tf = inverse * diag.T
        ew = mm(tf, w, THREE)
        e[g] = ew
        tb[g, :width] = tf
        bf = mm(w.T, jnp.concatenate([tf, ew], axis=1), THREE)
        tb[g, width:] = bf[:, :width]
        f[g] = bf[:, width:]

    @pl.when(first | last)
    def _():
        pl.semaphore_wait(bar, 5)

    @pl.when(jnp.logical_not(first | last))
    def _():
        pl.semaphore_wait(bar, 6)

    sent(0, 2).start()
    c0(0)
    sent(1, 2).start()
    c0(1)
    vh[...] = jnp.zeros_like(vh)
    vl[...] = jnp.zeros_like(vl)
    cc[...] = jnp.zeros_like(cc)
    grow[...] = jnp.zeros_like(grow)

    def up0(k):
        return pltpu.make_async_remote_copy(
            src_ref=xs.at[k],
            dst_ref=hin.at[0, k, pl.ds(B, B)],
            send_sem=s_up0.at[k],
            recv_sem=r_t.at[0, k],
            device_id={"row": row - 1},
            device_id_type=MESH,
        )

    def up(g, k):
        return pltpu.make_async_remote_copy(
            src_ref=hout.at[g, k, pl.ds(0, B)],
            dst_ref=hin.at[g + 1, k, pl.ds(B, B)],
            send_sem=s_up.at[g, k],
            recv_sem=r_t.at[g + 1, k],
            device_id={"row": row - 1},
            device_id_type=MESH,
        )

    def down(g, k):
        return pltpu.make_async_remote_copy(
            src_ref=hout.at[g, k, pl.ds(B, B)],
            dst_ref=hin.at[g, k, pl.ds(0, B)],
            send_sem=s_dn.at[g, k],
            recv_sem=r_h.at[g, k],
            device_id={"row": row + 1},
            device_id_type=MESH,
        )

    def recv_h(g, k):
        return pltpu.make_async_remote_copy(
            src_ref=hout.at[g, k, pl.ds(B, B)],
            dst_ref=hin.at[g, k, pl.ds(0, B)],
            send_sem=s_dn.at[g, k],
            recv_sem=r_h.at[g, k],
            device_id={"row": row - 1},
            device_id_type=MESH,
        )

    def recv_t(g, k):
        return pltpu.make_async_remote_copy(
            src_ref=xs.at[k],
            dst_ref=hin.at[g, k, pl.ds(B, B)],
            send_sem=s_up0.at[k],
            recv_sem=r_t.at[g, k],
            device_id={"row": row + 1},
            device_id_type=MESH,
        )

    x_copy.wait()
    for k in range(chunks):
        xs[k] = x[:B, k * part : (k + 1) * part]
        own[k] = xs[k]

    @pl.when(jnp.logical_not(first))
    def _():
        for k in range(chunks):
            up0(k).start()

    for g in range(2, groups):
        sent(g, 2).start()

    @pl.when(last)
    def _():
        for g in range(groups):
            for k in range(chunks):
                hin[g, k, B:] = jnp.zeros((B, part), jnp.float32)

    high, low = split(x[B:])
    xh[...] = high
    xl[...] = low
    c1(0)
    c0(2)
    c2(0)
    c1(1)
    x_back = pltpu.make_async_copy(x, x_out, xo_sem)
    v_back = (
        pltpu.make_async_copy(vh.at[groups - 1], vh_out, o_sem.at[0]),
        pltpu.make_async_copy(vl.at[groups - 1], vl_out, o_sem.at[1]),
    )
    lead = jnp.minimum(1 + row // 2, groups)

    def link(g, k):
        cols = slice(k * part, (k + 1) * part)

        @pl.when(jnp.logical_not(first))
        def _():
            recv_h(g, k).wait_recv()

        @pl.when(jnp.logical_not(last))
        def _():
            recv_t(g, k).wait_recv()

        top = jnp.where(first, own[k], hin[g, k, :B])
        h = jnp.concatenate([top, hin[g, k, B:]], axis=0)
        hn = (h - ty[B:, cols]) - mm(f[g], h, THREE)
        hout[g, k] = hn

        @pl.when(jnp.logical_not(last))
        def _():
            down(g, k).start()

        @pl.when(jnp.logical_not(first) & (g < groups - 1))
        def _():
            up(g, k).start()

        own[k] = hn[:B]
        cc[g, :, cols] = ty[:B, cols] + mm(e[g], h, THREE)

    def update(g, piece):
        size = (row_count - B) // 5
        high, low = split(cc[g])
        at = slice(piece * size, (piece + 1) * size)
        left = jnp.concatenate([vh[g, :, at], vl[g, :, at], vh[g, :, at]], axis=0)
        right = jnp.concatenate([high, high, low], axis=0)
        change = mdot(left, right, 0, 0)
        there = slice(B + piece * size, B + (piece + 1) * size)
        x[there] = x[there] - change

    def step(t, carry):
        def comm(move, g):
            @pl.when(g < groups)
            def _():
                move(g)

        comm(c3, t)
        comm(c0, t + 3)
        comm(c2, t + 1)
        comm(c1, t + 2)

        def chain(k):
            @pl.when((t >= lead) & (t < lead + groups))
            def _():
                link(t - lead, k)

        def work(piece):
            @pl.when(t < groups)
            def _():
                piece(t)

        def spread(*pieces):
            @pl.when((t > lead) & (t < lead + groups) & ((t >= groups) | (lead == 4)))
            def _():
                for piece in pieces:
                    update(t - lead - 1, piece)

        chain(0)
        work(c4)
        work(products)
        spread(0, 1)
        chain(1)
        work(grams)
        spread(2, 3)
        chain(2)
        spread(4)

        @pl.when(t == lead + groups - 1)
        def _():
            for back in v_back:
                back.start()

        @pl.when((t == lead + groups - 1) & (lead == 4))
        def _():
            x_back.start()

        work(factors)
        chain(3)

        @pl.when((t >= lead - 1) & (t < lead + groups - 1))
        def _():
            g = t - lead + 1
            whole = cc[...].reshape(groups * width, cc.shape[2])
            ty[...] = mm(tb[g], pm[g] - mm(grow[g], whole, THREE), THREE)

        return carry

    lax.fori_loop(0, lead + groups, step, 0)

    @pl.when(lead < 4)
    def _():
        def later(g, carry):
            for piece in range(5):
                update(g, piece)
            return carry

        lax.fori_loop(0, groups - 1 - lead, later, 0)
        x_back.start()

    c_out[...] = cc[groups - 1]
    for k in range(chunks):
        head_out[:, k * part : (k + 1) * part] = hout[groups - 1, k, :B]

    @pl.when(jnp.logical_not(first))
    def _():
        for k in range(chunks):
            up0(k).wait_send()

        def drain(g, carry):
            for k in range(chunks):
                up(g, k).wait_send()
            return carry

        lax.fori_loop(0, groups - 1, drain, 0)

    @pl.when(jnp.logical_not(last))
    def _():
        def drain(g, carry):
            for k in range(chunks):
                down(g, k).wait_send()
            return carry

        lax.fori_loop(0, groups, drain, 0)

    x_back.wait()
    for back in v_back:
        back.wait()
    for g in range(groups):
        for kind in range(9):
            sent(g, kind).wait_send()
        for mine in (True, False):
            for step in range(4):
                relay(g, mine, step).wait_send()


def fused(vin, ltau, live, x):
    groups, _, own, window = vin.shape
    lanes = window + B
    row_count, columns = x.shape
    mid = row_count - B
    part = columns // NC
    vm = pl.BlockSpec(memory_space=pltpu.VMEM)
    anywhere = pl.BlockSpec(memory_space=pl.ANY)
    small = pl.BlockSpec(memory_space=pltpu.SMEM)
    f32, b16 = jnp.float32, jnp.bfloat16
    shape = jax.ShapeDtypeStruct
    dma = pltpu.SemaphoreType.DMA
    return pl.pallas_call(
        fused_kernel,
        out_shape=(
            shape((row_count, columns), f32),
            shape((B, mid), b16),
            shape((B, mid), b16),
            shape((B, columns), f32),
            shape((B, columns), f32),
        ),
        in_specs=[vm, small, small, anywhere],
        out_specs=(anywhere, anywhere, anywhere, vm, vm),
        scratch_shapes=[
            pltpu.VMEM((row_count, columns), f32),
            pltpu.VMEM((groups, B, columns), f32),
            pltpu.VMEM((groups, B, lanes), f32),
            pltpu.VMEM((groups, B, mid), b16),
            pltpu.VMEM((groups, B, mid), b16),
            pltpu.VMEM((groups, B, 2 * B), f32),
            pltpu.VMEM((mid, columns), b16),
            pltpu.VMEM((mid, columns), b16),
            pltpu.VMEM((groups, B, columns), f32),
            pltpu.VMEM((groups, B, groups * B), f32),
            pltpu.VMEM((groups, 3 * B, B), f32),
            pltpu.VMEM((groups, B, 2 * B), f32),
            pltpu.VMEM((groups, 2 * B, 2 * B), f32),
            pltpu.VMEM((3 * B, columns), f32),
            pltpu.VMEM((groups, NC, 2 * B, part), f32),
            pltpu.VMEM((groups, NC, 2 * B, part), f32),
            pltpu.VMEM((NC, B, part), f32),
            pltpu.VMEM((NC, B, part), f32),
            dma((groups, 17)),
            dma((groups, 17)),
            dma((2,)),
            dma,
            dma,
            dma((NC,)),
            dma((groups, NC)),
            dma((groups, NC)),
            dma((groups, NC)),
            dma((groups, NC)),
        ],
        compiler_params=pltpu.CompilerParams(
            collective_id=0, has_side_effects=True, vmem_limit_bytes=60 << 20
        ),
        name="fused",
    )(vin, ltau, live, x)


def finish_kernel(vh_hbm, vl_hbm, c, head, x_hbm, out, x, vh, vl, ch, cl, sem, o_sem):
    pieces, size = x.shape[0], x.shape[1]

    def loads(i):
        cols = pl.ds(i * size, size)
        return (
            pltpu.make_async_copy(x_hbm.at[pl.ds(B + i * size, size)], x.at[i], sem.at[i, 0]),
            pltpu.make_async_copy(vh_hbm.at[:, cols], vh.at[:, cols], sem.at[i, 1]),
            pltpu.make_async_copy(vl_hbm.at[:, cols], vl.at[:, cols], sem.at[i, 2]),
        )

    def store(i):
        return pltpu.make_async_copy(x.at[i], out.at[pl.ds(B + i * size, size)], o_sem.at[i])

    for i in range(pieces):
        for load in loads(i):
            load.start()
    top = pltpu.make_async_copy(head, out.at[pl.ds(0, B)], o_sem.at[pieces])
    top.start()
    high, low = split(c[...])
    ch[...] = high
    cl[...] = low
    for i in range(pieces):
        for load in loads(i):
            load.wait()
        cols = slice(i * size, (i + 1) * size)
        high = vh[:, cols]
        low = vl[:, cols]
        left = jnp.concatenate([high, low, high], axis=0)
        right = jnp.concatenate([ch[...], ch[...], cl[...]], axis=0)
        x[i] = x[i] - mdot(left, right, 0, 0)
        store(i).start()
    top.wait()
    for i in range(pieces):
        store(i).wait()


def finish(vh, vl, c, head, x):
    width, mid = vh.shape
    pieces = 5
    size = mid // pieces
    columns = x.shape[1]
    vm = pl.BlockSpec(memory_space=pltpu.VMEM)
    anywhere = pl.BlockSpec(memory_space=pl.ANY)
    dma = pltpu.SemaphoreType.DMA
    return pl.pallas_call(
        finish_kernel,
        out_shape=jax.ShapeDtypeStruct(x.shape, x.dtype),
        in_specs=[anywhere, anywhere, vm, vm, anywhere],
        out_specs=anywhere,
        scratch_shapes=[
            pltpu.VMEM((pieces, size, columns), jnp.float32),
            pltpu.VMEM(vh.shape, jnp.bfloat16),
            pltpu.VMEM(vh.shape, jnp.bfloat16),
            pltpu.VMEM((width, columns), jnp.bfloat16),
            pltpu.VMEM((width, columns), jnp.bfloat16),
            dma((pieces, 3)),
            dma((pieces + 1,)),
        ],
        compiler_params=pltpu.CompilerParams(vmem_limit_bytes=56 << 20),
        name="finish",
    )(vh, vl, c, head, x)


def per_device(x, mirror_entries, tau, tallies):
    rest, vh, vl, c, head = fused(mirror_entries, tau, tallies[:, 0], x)
    return finish(vh, vl, c, head, rest)


def solution(mesh):
    in_specs = (P("row", "col"), P(None, "row", "col", None), P(None, "row", "col"), P(None, "row"))
    return jax.shard_map(
        per_device, mesh=mesh, in_specs=in_specs, out_specs=P("row", "col"), check_vma=False
    )
```

```python
import jax
import jax.numpy as jnp
from jax import lax
from jax.experimental import pallas as pl
from jax.experimental.pallas import tpu as pltpu
from jax.sharding import PartitionSpec as P

EXACT = lax.Precision.HIGHEST
THREE = lax.Precision.HIGH
MESH = pl.DeviceIdType.MESH
B = 128
NC = 4


def mm(a, b, precision, ca=1, cb=0):
    return lax.dot_general(
        a, b, (((ca,), (cb,)), ((), ())), precision=precision, preferred_element_type=jnp.float32
    )


def mdot(a, b, ca=1, cb=0):
    return lax.dot_general(a, b, (((ca,), (cb,)), ((), ())), preferred_element_type=jnp.float32)


def split(value):
    high = value.astype(jnp.bfloat16)
    return high, (value - high.astype(jnp.float32)).astype(jnp.bfloat16)


def fused_kernel(
    vin, ltau, counts, xhbm, x_out, vh_out, vl_out, c_out, head_out, x, cc, vbuf, vh, vl, wbuf, xh, xl, pm, grow, tb, e, f,
    ty, hin, hout, xs, own, s_sem, r_sem, o_sem, x_sem, xo_sem, s_up0, s_up, s_dn, r_h, r_t
):
    chunks, part = hin.shape[1], hin.shape[3]
    groups, width, lanes = vbuf.shape
    window = lanes - B
    row_count = x.shape[0]
    half = lanes // 2
    row, col = lax.axis_index("row"), lax.axis_index("col")
    rows = lax.axis_size("row")
    first, last = row == 0, row == rows - 1
    keep = (row != rows - 1).astype(jnp.float32)
    side, yy, core = col // 8, (col % 8) // 2, col % 2

    def shard(side_, y_):
        return side_ * 8 + (y_ % 4) * 2 + core

    other = 1 - side
    to_up = shard(side, yy + 1)
    to_down = shard(side, yy + 3)
    to_x = shard(other, yy)
    to_sib = col + 1 - 2 * core

    x_copy = pltpu.make_async_copy(xhbm, x, x_sem)
    x_copy.start()
    bar = pltpu.get_barrier_semaphore()
    for target in (to_up, to_down, to_x, to_sib):
        pl.semaphore_signal(bar, inc=1, device_id={"col": target}, device_id_type=MESH)

    @pl.when(jnp.logical_not(first))
    def _():
        pl.semaphore_signal(bar, inc=1, device_id={"row": row - 1}, device_id_type=MESH)

    @pl.when(jnp.logical_not(last))
    def _():
        pl.semaphore_signal(bar, inc=1, device_id={"row": row + 1}, device_id_type=MESH)

    def rows_of(owner):
        return pl.ds(pl.multiple_of(owner * 8, 8), 8)

    eighth = lax.broadcasted_iota(jnp.int32, (8, B), 0)
    for g in range(groups):
        vbuf[g, rows_of(col), :window] = vin[g, 0]
        scale = jnp.zeros((8, B), jnp.float32)
        for i in range(8):
            scale = jnp.where(eighth == i, ltau[g, 0, i], scale)
        vbuf[g, rows_of(col), window:] = scale

    def copy(g, kind, owner, target, part=None):
        span = pl.ds(0, lanes) if part is None else pl.ds(part * half, half)
        place = vbuf.at[g, rows_of(owner), span]
        return pltpu.make_async_remote_copy(
            src_ref=place,
            dst_ref=place,
            send_sem=s_sem.at[g, kind],
            recv_sem=r_sem.at[g, kind],
            device_id={"col": target},
            device_id_type=MESH,
        )

    def sent(g, kind):
        owner, target, part = (
            (col, to_up, None),
            (col, to_down, None),
            (col, to_x, None),
            (shard(side, yy + 3), to_up, 0),
            (shard(side, yy + 1), to_down, 1),
            (shard(other, yy), to_up, None),
            (shard(other, yy), to_down, None),
            (shard(other, yy + 3), to_up, 0),
            (shard(other, yy + 1), to_down, 1),
        )[kind]
        return copy(g, kind, owner, target, part)

    def got(g, kind):
        owner, part = (
            (shard(side, yy + 3), None),
            (shard(side, yy + 1), None),
            (shard(other, yy), None),
            (shard(side, yy + 2), 0),
            (shard(side, yy + 2), 1),
            (shard(other, yy + 3), None),
            (shard(other, yy + 1), None),
            (shard(other, yy + 2), 0),
            (shard(other, yy + 2), 1),
        )[kind]
        return copy(g, kind, owner, to_up, part)

    def relay(g, mine, step):
        owner = shard(side if mine else other, yy + step)
        return copy(g, (9 if mine else 13) + step, owner, to_sib)

    def relayed(g, mine, step):
        owner = shard(side if mine else other, yy + step) + 1 - 2 * core
        return copy(g, (9 if mine else 13) + step, owner, to_sib)

    def c0(g):
        for kind in (0, 1):
            sent(g, kind).start()
        relay(g, True, 0).start()

    def c1(g):
        got(g, 0).wait_recv()
        sent(g, 3).start()
        relay(g, True, 3).start()
        got(g, 1).wait_recv()
        sent(g, 4).start()
        relay(g, True, 1).start()
        got(g, 2).wait_recv()
        sent(g, 5).start()
        sent(g, 6).start()
        relay(g, False, 0).start()

    def c2(g):
        got(g, 5).wait_recv()
        sent(g, 7).start()
        relay(g, False, 3).start()
        got(g, 6).wait_recv()
        sent(g, 8).start()
        relay(g, False, 1).start()
        got(g, 3).wait_recv()
        got(g, 4).wait_recv()
        relay(g, True, 2).start()

    def c3(g):
        got(g, 7).wait_recv()
        got(g, 8).wait_recv()
        relay(g, False, 2).start()

    def c4(g):
        for mine in (True, False):
            for step in range(4):
                relayed(g, mine, step).wait_recv()

    def alive_of(g, size):
        at = lax.broadcasted_iota(jnp.int32, (width, size), 0)
        return (at < counts[g]).astype(jnp.float32)

    def products(g):
        alive = alive_of(g, 1)
        high, low = split(vbuf[g, :, B:row_count] * alive)
        vh[g] = high
        vl[g] = low
        wbuf[g, :, :B] = vbuf[g, :, :B] * alive
        wbuf[g, :, B:] = vbuf[g, :, row_count:window] * (alive * keep)
        both = mdot(jnp.concatenate([high, low], axis=0), xh[...])
        pm[g] = both[:width] + both[width:] + mdot(high, xl[...])

    def grams(g):
        def against(count):
            high, low = vh[g], vl[g]
            allh = vh[:count].reshape(count * width, row_count - B)
            alll = vl[:count].reshape(count * width, row_count - B)
            both = mdot(jnp.concatenate([high, low], axis=0), allh, 1, 1)
            grow[g, :, : count * width] = (
                both[:width] + both[width:] + mdot(high, alll, 1, 1)
            )

        for low_g, high_g in ((0, 1), (1, groups // 2), (groups // 2, groups)):

            @pl.when((g >= low_g) & (g < high_g))
            def _():
                against(high_g)

    def factors(g):
        row_at = lax.broadcasted_iota(jnp.int32, (width, width), 0)
        col_at = lax.broadcasted_iota(jnp.int32, (width, width), 1)
        eye = (row_at == col_at).astype(jnp.float32)
        alive = alive_of(g, width)
        w = wbuf[g]
        here = pl.ds(pl.multiple_of(g * width, width), width)
        gram = grow[g, :, here] + mm(w, w, EXACT, 1, 1)
        grow[g, :, here] = jnp.zeros((width, width), jnp.float32)
        diag = vbuf[g, :, window:] * alive + (1.0 - alive)
        power = jnp.where(col_at > row_at, -(diag * gram), 0.0)
        inverse = eye + power
        power = mm(power, power, THREE)
        reached = 2
        while reached < width:
            if 2 * reached < width:
                both = mm(jnp.concatenate([power, inverse], axis=0), power, THREE)
                power = both[:width]
                inverse = inverse + both[width:]
            else:
                inverse = inverse + mm(inverse, power, THREE)
            reached = reached * 2
        tf = inverse * diag.T
        ew = mm(tf, w, THREE)
        e[g] = ew
        tb[g, :width] = tf
        bf = mm(w.T, jnp.concatenate([tf, ew], axis=1), THREE)
        tb[g, width:] = bf[:, :width]
        f[g] = bf[:, width:]

    @pl.when(first | last)
    def _():
        pl.semaphore_wait(bar, 5)

    @pl.when(jnp.logical_not(first | last))
    def _():
        pl.semaphore_wait(bar, 6)

    sent(0, 2).start()
    c0(0)
    sent(1, 2).start()
    c0(1)
    vh[...] = jnp.zeros_like(vh)
    vl[...] = jnp.zeros_like(vl)
    cc[...] = jnp.zeros_like(cc)
    grow[...] = jnp.zeros_like(grow)

    def up0(k):
        return pltpu.make_async_remote_copy(
            src_ref=xs.at[k],
            dst_ref=hin.at[0, k, pl.ds(B, B)],
            send_sem=s_up0.at[k],
            recv_sem=r_t.at[0, k],
            device_id={"row": row - 1},
            device_id_type=MESH,
        )

    def up(g, k):
        return pltpu.make_async_remote_copy(
            src_ref=hout.at[g, k, pl.ds(0, B)],
            dst_ref=hin.at[g + 1, k, pl.ds(B, B)],
            send_sem=s_up.at[g, k],
            recv_sem=r_t.at[g + 1, k],
            device_id={"row": row - 1},
            device_id_type=MESH,
        )

    def down(g, k):
        return pltpu.make_async_remote_copy(
            src_ref=hout.at[g, k, pl.ds(B, B)],
            dst_ref=hin.at[g, k, pl.ds(0, B)],
            send_sem=s_dn.at[g, k],
            recv_sem=r_h.at[g, k],
            device_id={"row": row + 1},
            device_id_type=MESH,
        )

    def recv_h(g, k):
        return pltpu.make_async_remote_copy(
            src_ref=hout.at[g, k, pl.ds(B, B)],
            dst_ref=hin.at[g, k, pl.ds(0, B)],
            send_sem=s_dn.at[g, k],
            recv_sem=r_h.at[g, k],
            device_id={"row": row - 1},
            device_id_type=MESH,
        )

    def recv_t(g, k):
        return pltpu.make_async_remote_copy(
            src_ref=xs.at[k],
            dst_ref=hin.at[g, k, pl.ds(B, B)],
            send_sem=s_up0.at[k],
            recv_sem=r_t.at[g, k],
            device_id={"row": row + 1},
            device_id_type=MESH,
        )

    x_copy.wait()
    for k in range(chunks):
        xs[k] = x[:B, k * part : (k + 1) * part]
        own[k] = xs[k]

    @pl.when(jnp.logical_not(first))
    def _():
        for k in range(chunks):
            up0(k).start()

    for g in range(2, groups):
        sent(g, 2).start()

    @pl.when(last)
    def _():
        for g in range(groups):
            for k in range(chunks):
                hin[g, k, B:] = jnp.zeros((B, part), jnp.float32)

    high, low = split(x[B:])
    xh[...] = high
    xl[...] = low
    c1(0)
    c0(2)
    c2(0)
    c1(1)
    x_back = pltpu.make_async_copy(x, x_out, xo_sem)
    v_back = (
        pltpu.make_async_copy(vh.at[groups - 1], vh_out, o_sem.at[0]),
        pltpu.make_async_copy(vl.at[groups - 1], vl_out, o_sem.at[1]),
    )
    lead = 1 + row // 3

    def link(g, k):
        cols = slice(k * part, (k + 1) * part)

        @pl.when(jnp.logical_not(first))
        def _():
            recv_h(g, k).wait_recv()

        @pl.when(jnp.logical_not(last))
        def _():
            recv_t(g, k).wait_recv()

        top = jnp.where(first, own[k], hin[g, k, :B])
        h = jnp.concatenate([top, hin[g, k, B:]], axis=0)
        hn = (h - ty[B:, cols]) - mm(f[g], h, THREE)
        hout[g, k] = hn

        @pl.when(jnp.logical_not(last))
        def _():
            down(g, k).start()

        @pl.when(jnp.logical_not(first) & (g < groups - 1))
        def _():
            up(g, k).start()

        own[k] = hn[:B]
        cc[g, :, cols] = ty[:B, cols] + mm(e[g], h, THREE)

    def update(g, piece):
        size = (row_count - B) // 5
        high, low = split(cc[g])
        at = slice(piece * size, (piece + 1) * size)
        left = jnp.concatenate([vh[g, :, at], vl[g, :, at], vh[g, :, at]], axis=0)
        right = jnp.concatenate([high, high, low], axis=0)
        change = mdot(left, right, 0, 0)
        there = slice(B + piece * size, B + (piece + 1) * size)
        x[there] = x[there] - change

    def step(t, carry):
        def comm(move, g):
            @pl.when(g < groups)
            def _():
                move(g)

        comm(c3, t)
        comm(c0, t + 3)
        comm(c2, t + 1)
        comm(c1, t + 2)

        def chain(k):
            @pl.when((t >= lead) & (t < lead + groups))
            def _():
                link(t - lead, k)

        def work(piece):
            @pl.when(t < groups)
            def _():
                piece(t)

        def spread(*pieces):
            @pl.when((t > lead) & (t < lead + groups) & ((t >= groups) | (row >= 6)))
            def _():
                for piece in pieces:
                    update(t - lead - 1, piece)

        chain(0)
        work(c4)
        work(products)
        spread(0, 1)
        chain(1)
        work(grams)
        spread(2, 3)
        chain(2)
        spread(4)

        @pl.when(t == lead + groups - 1)
        def _():
            for back in v_back:
                back.start()

        @pl.when((t == lead + groups - 1) & (row >= 6))
        def _():
            x_back.start()

        work(factors)
        chain(3)

        @pl.when((t >= lead - 1) & (t < lead + groups - 1))
        def _():
            g = t - lead + 1
            whole = cc[...].reshape(groups * width, cc.shape[2])
            ty[...] = mm(tb[g], pm[g] - mm(grow[g], whole, THREE), THREE)

        return carry

    lax.fori_loop(0, lead + groups, step, 0)

    @pl.when(row < 6)
    def _():
        def later(g, carry):
            for piece in range(5):
                update(g, piece)
            return carry

        lax.fori_loop(0, groups - 1 - lead, later, 0)
        x_back.start()

    c_out[...] = cc[groups - 1]
    for k in range(chunks):
        head_out[:, k * part : (k + 1) * part] = hout[groups - 1, k, :B]

    @pl.when(jnp.logical_not(first))
    def _():
        for k in range(chunks):
            up0(k).wait_send()

        def drain(g, carry):
            for k in range(chunks):
                up(g, k).wait_send()
            return carry

        lax.fori_loop(0, groups - 1, drain, 0)

    @pl.when(jnp.logical_not(last))
    def _():
        def drain(g, carry):
            for k in range(chunks):
                down(g, k).wait_send()
            return carry

        lax.fori_loop(0, groups, drain, 0)

    x_back.wait()
    for back in v_back:
        back.wait()
    for g in range(groups):
        for kind in range(9):
            sent(g, kind).wait_send()
        for mine in (True, False):
            for step in range(4):
                relay(g, mine, step).wait_send()


def fused(vin, ltau, live, x):
    groups, _, own, window = vin.shape
    lanes = window + B
    row_count, columns = x.shape
    mid = row_count - B
    part = columns // NC
    vm = pl.BlockSpec(memory_space=pltpu.VMEM)
    anywhere = pl.BlockSpec(memory_space=pl.ANY)
    small = pl.BlockSpec(memory_space=pltpu.SMEM)
    f32, b16 = jnp.float32, jnp.bfloat16
    shape = jax.ShapeDtypeStruct
    dma = pltpu.SemaphoreType.DMA
    return pl.pallas_call(
        fused_kernel,
        out_shape=(
            shape((row_count, columns), f32),
            shape((B, mid), b16),
            shape((B, mid), b16),
            shape((B, columns), f32),
            shape((B, columns), f32),
        ),
        in_specs=[vm, small, small, anywhere],
        out_specs=(anywhere, anywhere, anywhere, vm, vm),
        scratch_shapes=[
            pltpu.VMEM((row_count, columns), f32),
            pltpu.VMEM((groups, B, columns), f32),
            pltpu.VMEM((groups, B, lanes), f32),
            pltpu.VMEM((groups, B, mid), b16),
            pltpu.VMEM((groups, B, mid), b16),
            pltpu.VMEM((groups, B, 2 * B), f32),
            pltpu.VMEM((mid, columns), b16),
            pltpu.VMEM((mid, columns), b16),
            pltpu.VMEM((groups, B, columns), f32),
            pltpu.VMEM((groups, B, groups * B), f32),
            pltpu.VMEM((groups, 3 * B, B), f32),
            pltpu.VMEM((groups, B, 2 * B), f32),
            pltpu.VMEM((groups, 2 * B, 2 * B), f32),
            pltpu.VMEM((3 * B, columns), f32),
            pltpu.VMEM((groups, NC, 2 * B, part), f32),
            pltpu.VMEM((groups, NC, 2 * B, part), f32),
            pltpu.VMEM((NC, B, part), f32),
            pltpu.VMEM((NC, B, part), f32),
            dma((groups, 17)),
            dma((groups, 17)),
            dma((2,)),
            dma,
            dma,
            dma((NC,)),
            dma((groups, NC)),
            dma((groups, NC)),
            dma((groups, NC)),
            dma((groups, NC)),
        ],
        compiler_params=pltpu.CompilerParams(
            collective_id=0, has_side_effects=True, vmem_limit_bytes=60 << 20
        ),
        name="fused",
    )(vin, ltau, live, x)


def finish_kernel(vh_hbm, vl_hbm, c, head, x_hbm, out, x, vh, vl, ch, cl, sem, o_sem):
    pieces, size = x.shape[0], x.shape[1]

    def loads(i):
        cols = pl.ds(i * size, size)
        return (
            pltpu.make_async_copy(x_hbm.at[pl.ds(B + i * size, size)], x.at[i], sem.at[i, 0]),
            pltpu.make_async_copy(vh_hbm.at[:, cols], vh.at[:, cols], sem.at[i, 1]),
            pltpu.make_async_copy(vl_hbm.at[:, cols], vl.at[:, cols], sem.at[i, 2]),
        )

    def store(i):
        return pltpu.make_async_copy(x.at[i], out.at[pl.ds(B + i * size, size)], o_sem.at[i])

    for i in range(pieces):
        for load in loads(i):
            load.start()
    top = pltpu.make_async_copy(head, out.at[pl.ds(0, B)], o_sem.at[pieces])
    top.start()
    high, low = split(c[...])
    ch[...] = high
    cl[...] = low
    for i in range(pieces):
        for load in loads(i):
            load.wait()
        cols = slice(i * size, (i + 1) * size)
        high = vh[:, cols]
        low = vl[:, cols]
        left = jnp.concatenate([high, low, high], axis=0)
        right = jnp.concatenate([ch[...], ch[...], cl[...]], axis=0)
        x[i] = x[i] - mdot(left, right, 0, 0)
        store(i).start()
    top.wait()
    for i in range(pieces):
        store(i).wait()


def finish(vh, vl, c, head, x):
    width, mid = vh.shape
    pieces = 5
    size = mid // pieces
    columns = x.shape[1]
    vm = pl.BlockSpec(memory_space=pltpu.VMEM)
    anywhere = pl.BlockSpec(memory_space=pl.ANY)
    dma = pltpu.SemaphoreType.DMA
    return pl.pallas_call(
        finish_kernel,
        out_shape=jax.ShapeDtypeStruct(x.shape, x.dtype),
        in_specs=[anywhere, anywhere, vm, vm, anywhere],
        out_specs=anywhere,
        scratch_shapes=[
            pltpu.VMEM((pieces, size, columns), jnp.float32),
            pltpu.VMEM(vh.shape, jnp.bfloat16),
            pltpu.VMEM(vh.shape, jnp.bfloat16),
            pltpu.VMEM((width, columns), jnp.bfloat16),
            pltpu.VMEM((width, columns), jnp.bfloat16),
            dma((pieces, 3)),
            dma((pieces + 1,)),
        ],
        compiler_params=pltpu.CompilerParams(vmem_limit_bytes=56 << 20),
        name="finish",
    )(vh, vl, c, head, x)


def per_device(x, mirror_entries, tau, tallies):
    rest, vh, vl, c, head = fused(mirror_entries, tau, tallies[:, 0], x)
    return finish(vh, vl, c, head, rest)


def solution(mesh):
    in_specs = (P("row", "col"), P(None, "row", "col", None), P(None, "row", "col"), P(None, "row"))
    return jax.shard_map(
        per_device, mesh=mesh, in_specs=in_specs, out_specs=P("row", "col"), check_vma=False
    )
```

```python
import jax
import jax.numpy as jnp
from jax import lax
from jax.experimental import pallas as pl
from jax.experimental.pallas import tpu as pltpu
from jax.sharding import PartitionSpec as P

THREE = lax.Precision.HIGH
MESH = pl.DeviceIdType.MESH
B = 128
NC = 4


def mm(a, b, precision, ca=1, cb=0):
    return lax.dot_general(
        a, b, (((ca,), (cb,)), ((), ())), precision=precision, preferred_element_type=jnp.float32
    )


def mdot(a, b, ca=1, cb=0):
    return lax.dot_general(a, b, (((ca,), (cb,)), ((), ())), preferred_element_type=jnp.float32)


def split(value):
    high = value.astype(jnp.bfloat16)
    return high, (value - high.astype(jnp.float32)).astype(jnp.bfloat16)


def fused_kernel(
    vin, ltau, counts, xhbm, x_out, vh_out, vl_out, c_out, head_out, x, cc, vbuf, vh, vl, wbuf, xh, xl, pm, grow, tb, e, f,
    ty, hin, hout, xs, own, s_sem, r_sem, o_sem, x_sem, xo_sem, s_up0, s_up, s_dn, r_h, r_t
):
    chunks, part = hin.shape[1], hin.shape[3]
    groups, width, lanes = vbuf.shape
    window = lanes - B
    row_count = x.shape[0]
    half = lanes // 2
    row, col = lax.axis_index("row"), lax.axis_index("col")
    rows = lax.axis_size("row")
    first, last = row == 0, row == rows - 1
    keep = (row != rows - 1).astype(jnp.float32)
    side, yy, core = col // 8, (col % 8) // 2, col % 2

    def shard(side_, y_):
        return side_ * 8 + (y_ % 4) * 2 + core

    other = 1 - side
    to_up = shard(side, yy + 1)
    to_down = shard(side, yy + 3)
    to_x = shard(other, yy)
    to_sib = col + 1 - 2 * core

    x_copy = pltpu.make_async_copy(xhbm, x, x_sem)
    x_copy.start()
    bar = pltpu.get_barrier_semaphore()
    for target in (to_up, to_down, to_x, to_sib):
        pl.semaphore_signal(bar, inc=1, device_id={"col": target}, device_id_type=MESH)

    @pl.when(jnp.logical_not(first))
    def _():
        pl.semaphore_signal(bar, inc=1, device_id={"row": row - 1}, device_id_type=MESH)

    @pl.when(jnp.logical_not(last))
    def _():
        pl.semaphore_signal(bar, inc=1, device_id={"row": row + 1}, device_id_type=MESH)

    def rows_of(owner):
        return pl.ds(pl.multiple_of(owner * 8, 8), 8)

    eighth = lax.broadcasted_iota(jnp.int32, (8, B), 0)
    for g in range(groups):
        vbuf[g, rows_of(col), :window] = vin[g, 0]
        scale = jnp.zeros((8, B), jnp.float32)
        for i in range(8):
            scale = jnp.where(eighth == i, ltau[g, 0, i], scale)
        vbuf[g, rows_of(col), window:] = scale

    def copy(g, kind, owner, target, part=None):
        span = pl.ds(0, lanes) if part is None else pl.ds(part * half, half)
        place = vbuf.at[g, rows_of(owner), span]
        return pltpu.make_async_remote_copy(
            src_ref=place,
            dst_ref=place,
            send_sem=s_sem.at[g, kind],
            recv_sem=r_sem.at[g, kind],
            device_id={"col": target},
            device_id_type=MESH,
        )

    def sent(g, kind):
        owner, target, part = (
            (col, to_up, None),
            (col, to_down, None),
            (col, to_x, None),
            (shard(side, yy + 3), to_up, 0),
            (shard(side, yy + 1), to_down, 1),
            (shard(other, yy), to_up, None),
            (shard(other, yy), to_down, None),
            (shard(other, yy + 3), to_up, 0),
            (shard(other, yy + 1), to_down, 1),
        )[kind]
        return copy(g, kind, owner, target, part)

    def got(g, kind):
        owner, part = (
            (shard(side, yy + 3), None),
            (shard(side, yy + 1), None),
            (shard(other, yy), None),
            (shard(side, yy + 2), 0),
            (shard(side, yy + 2), 1),
            (shard(other, yy + 3), None),
            (shard(other, yy + 1), None),
            (shard(other, yy + 2), 0),
            (shard(other, yy + 2), 1),
        )[kind]
        return copy(g, kind, owner, to_up, part)

    def relay(g, mine, step):
        owner = shard(side if mine else other, yy + step)
        return copy(g, (9 if mine else 13) + step, owner, to_sib)

    def relayed(g, mine, step):
        owner = shard(side if mine else other, yy + step) + 1 - 2 * core
        return copy(g, (9 if mine else 13) + step, owner, to_sib)

    def c0(g):
        for kind in (0, 1):
            sent(g, kind).start()
        relay(g, True, 0).start()

    def c1(g):
        got(g, 0).wait_recv()
        sent(g, 3).start()
        relay(g, True, 3).start()
        got(g, 1).wait_recv()
        sent(g, 4).start()
        relay(g, True, 1).start()
        got(g, 2).wait_recv()
        sent(g, 5).start()
        sent(g, 6).start()
        relay(g, False, 0).start()

    def c2(g):
        got(g, 5).wait_recv()
        sent(g, 7).start()
        relay(g, False, 3).start()
        got(g, 6).wait_recv()
        sent(g, 8).start()
        relay(g, False, 1).start()
        got(g, 3).wait_recv()
        got(g, 4).wait_recv()
        relay(g, True, 2).start()

    def c3(g):
        got(g, 7).wait_recv()
        got(g, 8).wait_recv()
        relay(g, False, 2).start()

    def c4(g):
        for mine in (True, False):
            for step in range(4):
                relayed(g, mine, step).wait_recv()

    def alive_of(g, size):
        at = lax.broadcasted_iota(jnp.int32, (width, size), 0)
        return (at < counts[g]).astype(jnp.float32)

    def products(g):
        alive = alive_of(g, 1)
        high, low = split(vbuf[g, :, B:row_count] * alive)
        vh[g] = high
        vl[g] = low
        wbuf[g, :, :B] = vbuf[g, :, :B] * alive
        wbuf[g, :, B:] = vbuf[g, :, row_count:window] * (alive * keep)
        both = mdot(jnp.concatenate([high, low], axis=0), xh[...])
        pm[g] = both[:width] + both[width:] + mdot(high, xl[...])

    def grams(g):
        def against(count):
            high, low = vh[g], vl[g]
            allh = vh[:count].reshape(count * width, row_count - B)
            alll = vl[:count].reshape(count * width, row_count - B)
            both = mdot(jnp.concatenate([high, low], axis=0), allh, 1, 1)
            grow[g, :, : count * width] = (
                both[:width] + both[width:] + mdot(high, alll, 1, 1)
            )

        for low_g, high_g in ((0, 1), (1, groups // 2), (groups // 2, groups)):

            @pl.when((g >= low_g) & (g < high_g))
            def _():
                against(high_g)

    def factors(g):
        row_at = lax.broadcasted_iota(jnp.int32, (width, width), 0)
        col_at = lax.broadcasted_iota(jnp.int32, (width, width), 1)
        eye = (row_at == col_at).astype(jnp.float32)
        alive = alive_of(g, width)
        w = wbuf[g]
        here = pl.ds(pl.multiple_of(g * width, width), width)
        gram = grow[g, :, here] + mm(w, w, THREE, 1, 1)
        grow[g, :, here] = jnp.zeros((width, width), jnp.float32)
        diag = vbuf[g, :, window:] * alive + (1.0 - alive)
        power = jnp.where(col_at > row_at, -(diag * gram), 0.0)
        inverse = eye + power
        power = mm(power, power, THREE)
        reached = 2
        while reached < width:
            if 2 * reached < width:
                both = mm(jnp.concatenate([power, inverse], axis=0), power, THREE)
                power = both[:width]
                inverse = inverse + both[width:]
            else:
                inverse = inverse + mm(inverse, power, THREE)
            reached = reached * 2
        tf = inverse * diag.T
        ew = mm(tf, w, THREE)
        e[g] = ew
        tb[g, :width] = tf
        bf = mm(w.T, jnp.concatenate([tf, ew], axis=1), THREE)
        tb[g, width:] = bf[:, :width]
        f[g] = bf[:, width:]

    @pl.when(first | last)
    def _():
        pl.semaphore_wait(bar, 5)

    @pl.when(jnp.logical_not(first | last))
    def _():
        pl.semaphore_wait(bar, 6)

    sent(0, 2).start()
    c0(0)
    sent(1, 2).start()
    c0(1)
    vh[...] = jnp.zeros_like(vh)
    vl[...] = jnp.zeros_like(vl)
    cc[...] = jnp.zeros_like(cc)
    grow[...] = jnp.zeros_like(grow)

    def up0(k):
        return pltpu.make_async_remote_copy(
            src_ref=xs.at[k],
            dst_ref=hin.at[0, k, pl.ds(B, B)],
            send_sem=s_up0.at[k],
            recv_sem=r_t.at[0, k],
            device_id={"row": row - 1},
            device_id_type=MESH,
        )

    def up(g, k):
        return pltpu.make_async_remote_copy(
            src_ref=hout.at[g, k, pl.ds(0, B)],
            dst_ref=hin.at[g + 1, k, pl.ds(B, B)],
            send_sem=s_up.at[g, k],
            recv_sem=r_t.at[g + 1, k],
            device_id={"row": row - 1},
            device_id_type=MESH,
        )

    def down(g, k):
        return pltpu.make_async_remote_copy(
            src_ref=hout.at[g, k, pl.ds(B, B)],
            dst_ref=hin.at[g, k, pl.ds(0, B)],
            send_sem=s_dn.at[g, k],
            recv_sem=r_h.at[g, k],
            device_id={"row": row + 1},
            device_id_type=MESH,
        )

    def recv_h(g, k):
        return pltpu.make_async_remote_copy(
            src_ref=hout.at[g, k, pl.ds(B, B)],
            dst_ref=hin.at[g, k, pl.ds(0, B)],
            send_sem=s_dn.at[g, k],
            recv_sem=r_h.at[g, k],
            device_id={"row": row - 1},
            device_id_type=MESH,
        )

    def recv_t(g, k):
        return pltpu.make_async_remote_copy(
            src_ref=xs.at[k],
            dst_ref=hin.at[g, k, pl.ds(B, B)],
            send_sem=s_up0.at[k],
            recv_sem=r_t.at[g, k],
            device_id={"row": row + 1},
            device_id_type=MESH,
        )

    x_copy.wait()
    for k in range(chunks):
        xs[k] = x[:B, k * part : (k + 1) * part]
        own[k] = xs[k]

    @pl.when(jnp.logical_not(first))
    def _():
        for k in range(chunks):
            up0(k).start()

    for g in range(2, groups):
        sent(g, 2).start()

    @pl.when(last)
    def _():
        for g in range(groups):
            for k in range(chunks):
                hin[g, k, B:] = jnp.zeros((B, part), jnp.float32)

    high, low = split(x[B:])
    xh[...] = high
    xl[...] = low
    c1(0)
    c0(2)
    c2(0)
    c1(1)
    x_back = pltpu.make_async_copy(x, x_out, xo_sem)
    v_back = (
        pltpu.make_async_copy(vh.at[groups - 1], vh_out, o_sem.at[0]),
        pltpu.make_async_copy(vl.at[groups - 1], vl_out, o_sem.at[1]),
    )
    lead = 1 + row // 3

    def link(g, k):
        cols = slice(k * part, (k + 1) * part)

        @pl.when(jnp.logical_not(first))
        def _():
            recv_h(g, k).wait_recv()

        @pl.when(jnp.logical_not(last))
        def _():
            recv_t(g, k).wait_recv()

        top = jnp.where(first, own[k], hin[g, k, :B])
        h = jnp.concatenate([top, hin[g, k, B:]], axis=0)
        hn = (h - ty[B:, cols]) - mm(f[g], h, THREE)
        hout[g, k] = hn

        @pl.when(jnp.logical_not(last))
        def _():
            down(g, k).start()

        @pl.when(jnp.logical_not(first) & (g < groups - 1))
        def _():
            up(g, k).start()

        own[k] = hn[:B]
        cc[g, :, cols] = ty[:B, cols] + mm(e[g], h, THREE)

    def update(g, piece):
        size = (row_count - B) // 5
        high, low = split(cc[g])
        at = slice(piece * size, (piece + 1) * size)
        left = jnp.concatenate([vh[g, :, at], vl[g, :, at], vh[g, :, at]], axis=0)
        right = jnp.concatenate([high, high, low], axis=0)
        change = mdot(left, right, 0, 0)
        there = slice(B + piece * size, B + (piece + 1) * size)
        x[there] = x[there] - change

    def step(t, carry):
        def comm(move, g):
            @pl.when(g < groups)
            def _():
                move(g)

        comm(c3, t)
        comm(c0, t + 3)
        comm(c2, t + 1)
        comm(c1, t + 2)

        def chain(k):
            @pl.when((t >= lead) & (t < lead + groups))
            def _():
                link(t - lead, k)

        def work(piece):
            @pl.when(t < groups)
            def _():
                piece(t)

        def spread(*pieces):
            @pl.when((t > lead) & (t < lead + groups) & ((t >= groups) | (row >= 6)))
            def _():
                for piece in pieces:
                    update(t - lead - 1, piece)

        chain(0)
        work(c4)
        work(products)
        spread(0, 1)
        chain(1)
        work(grams)
        spread(2, 3)
        chain(2)
        spread(4)

        @pl.when(t == lead + groups - 1)
        def _():
            for back in v_back:
                back.start()

        @pl.when((t == lead + groups - 1) & (row >= 6))
        def _():
            x_back.start()

        work(factors)
        chain(3)

        @pl.when((t >= lead - 1) & (t < lead + groups - 1))
        def _():
            g = t - lead + 1
            whole = cc[...].reshape(groups * width, cc.shape[2])
            ty[...] = mm(tb[g], pm[g] - mm(grow[g], whole, THREE), THREE)

        return carry

    lax.fori_loop(0, lead + groups, step, 0)

    @pl.when(row < 6)
    def _():
        def later(g, carry):
            for piece in range(5):
                update(g, piece)
            return carry

        lax.fori_loop(0, groups - 1 - lead, later, 0)
        x_back.start()

    c_out[...] = cc[groups - 1]
    for k in range(chunks):
        head_out[:, k * part : (k + 1) * part] = hout[groups - 1, k, :B]

    @pl.when(jnp.logical_not(first))
    def _():
        for k in range(chunks):
            up0(k).wait_send()

        def drain(g, carry):
            for k in range(chunks):
                up(g, k).wait_send()
            return carry

        lax.fori_loop(0, groups - 1, drain, 0)

    @pl.when(jnp.logical_not(last))
    def _():
        def drain(g, carry):
            for k in range(chunks):
                down(g, k).wait_send()
            return carry

        lax.fori_loop(0, groups, drain, 0)

    x_back.wait()
    for back in v_back:
        back.wait()
    for g in range(groups):
        for kind in range(9):
            sent(g, kind).wait_send()
        for mine in (True, False):
            for step in range(4):
                relay(g, mine, step).wait_send()


def fused(vin, ltau, live, x):
    groups, _, own, window = vin.shape
    lanes = window + B
    row_count, columns = x.shape
    mid = row_count - B
    part = columns // NC
    vm = pl.BlockSpec(memory_space=pltpu.VMEM)
    anywhere = pl.BlockSpec(memory_space=pl.ANY)
    small = pl.BlockSpec(memory_space=pltpu.SMEM)
    f32, b16 = jnp.float32, jnp.bfloat16
    shape = jax.ShapeDtypeStruct
    dma = pltpu.SemaphoreType.DMA
    return pl.pallas_call(
        fused_kernel,
        out_shape=(
            shape((row_count, columns), f32),
            shape((B, mid), b16),
            shape((B, mid), b16),
            shape((B, columns), f32),
            shape((B, columns), f32),
        ),
        in_specs=[vm, small, small, anywhere],
        out_specs=(anywhere, anywhere, anywhere, vm, vm),
        scratch_shapes=[
            pltpu.VMEM((row_count, columns), f32),
            pltpu.VMEM((groups, B, columns), f32),
            pltpu.VMEM((groups, B, lanes), f32),
            pltpu.VMEM((groups, B, mid), b16),
            pltpu.VMEM((groups, B, mid), b16),
            pltpu.VMEM((groups, B, 2 * B), f32),
            pltpu.VMEM((mid, columns), b16),
            pltpu.VMEM((mid, columns), b16),
            pltpu.VMEM((groups, B, columns), f32),
            pltpu.VMEM((groups, B, groups * B), f32),
            pltpu.VMEM((groups, 3 * B, B), f32),
            pltpu.VMEM((groups, B, 2 * B), f32),
            pltpu.VMEM((groups, 2 * B, 2 * B), f32),
            pltpu.VMEM((3 * B, columns), f32),
            pltpu.VMEM((groups, NC, 2 * B, part), f32),
            pltpu.VMEM((groups, NC, 2 * B, part), f32),
            pltpu.VMEM((NC, B, part), f32),
            pltpu.VMEM((NC, B, part), f32),
            dma((groups, 17)),
            dma((groups, 17)),
            dma((2,)),
            dma,
            dma,
            dma((NC,)),
            dma((groups, NC)),
            dma((groups, NC)),
            dma((groups, NC)),
            dma((groups, NC)),
        ],
        compiler_params=pltpu.CompilerParams(
            collective_id=0, has_side_effects=True, vmem_limit_bytes=60 << 20
        ),
        name="fused",
    )(vin, ltau, live, x)


def finish_kernel(vh_hbm, vl_hbm, c, head, x_hbm, out, x, vh, vl, ch, cl, sem, o_sem):
    pieces, size = x.shape[0], x.shape[1]

    def loads(i):
        cols = pl.ds(i * size, size)
        return (
            pltpu.make_async_copy(x_hbm.at[pl.ds(B + i * size, size)], x.at[i], sem.at[i, 0]),
            pltpu.make_async_copy(vh_hbm.at[:, cols], vh.at[:, cols], sem.at[i, 1]),
            pltpu.make_async_copy(vl_hbm.at[:, cols], vl.at[:, cols], sem.at[i, 2]),
        )

    def store(i):
        return pltpu.make_async_copy(x.at[i], out.at[pl.ds(B + i * size, size)], o_sem.at[i])

    for i in range(pieces):
        for load in loads(i):
            load.start()
    top = pltpu.make_async_copy(head, out.at[pl.ds(0, B)], o_sem.at[pieces])
    top.start()
    high, low = split(c[...])
    ch[...] = high
    cl[...] = low
    for i in range(pieces):
        for load in loads(i):
            load.wait()
        cols = slice(i * size, (i + 1) * size)
        high = vh[:, cols]
        low = vl[:, cols]
        left = jnp.concatenate([high, low, high], axis=0)
        right = jnp.concatenate([ch[...], ch[...], cl[...]], axis=0)
        x[i] = x[i] - mdot(left, right, 0, 0)
        store(i).start()
    top.wait()
    for i in range(pieces):
        store(i).wait()


def finish(vh, vl, c, head, x):
    width, mid = vh.shape
    pieces = 5
    size = mid // pieces
    columns = x.shape[1]
    vm = pl.BlockSpec(memory_space=pltpu.VMEM)
    anywhere = pl.BlockSpec(memory_space=pl.ANY)
    dma = pltpu.SemaphoreType.DMA
    return pl.pallas_call(
        finish_kernel,
        out_shape=jax.ShapeDtypeStruct(x.shape, x.dtype),
        in_specs=[anywhere, anywhere, vm, vm, anywhere],
        out_specs=anywhere,
        scratch_shapes=[
            pltpu.VMEM((pieces, size, columns), jnp.float32),
            pltpu.VMEM(vh.shape, jnp.bfloat16),
            pltpu.VMEM(vh.shape, jnp.bfloat16),
            pltpu.VMEM((width, columns), jnp.bfloat16),
            pltpu.VMEM((width, columns), jnp.bfloat16),
            dma((pieces, 3)),
            dma((pieces + 1,)),
        ],
        compiler_params=pltpu.CompilerParams(vmem_limit_bytes=56 << 20),
        name="finish",
    )(vh, vl, c, head, x)


def per_device(x, mirror_entries, tau, tallies):
    rest, vh, vl, c, head = fused(mirror_entries, tau, tallies[:, 0], x)
    return finish(vh, vl, c, head, rest)


def solution(mesh):
    in_specs = (P("row", "col"), P(None, "row", "col", None), P(None, "row", "col"), P(None, "row"))
    return jax.shard_map(
        per_device, mesh=mesh, in_specs=in_specs, out_specs=P("row", "col"), check_vma=False
    )
```
